128 devices in a mesh: frame: 8 (over y_hi, z), batch: 16 (over x, y_lo, core).
Axes of the slice: x: 4, y: 4 (y_hi: 2, y_lo: 2; y = y_hi * 2 + y_lo), z: 4, core: 2. Of those that a mesh axis runs over, the one named last changes fastest.
Arguments:
- queries: bfloat16 [16, 1024, 5120], P('batch', 'frame'), may hold values from -180 to 180
- keys: bfloat16 [16, 1024, 5120], P('batch', 'frame'), may hold values from -6 to 6
- values: bfloat16 [16, 1024, 5120], P('batch', 'frame'), may hold values from -24 to 24
- out_weight: bfloat16 [5120, 5120], P(None, 'batch'), may hold values from -0.078125 to 0.078125
- gate: float32 [16, 5120], P('batch'), may hold values from -6 to 6
- kv_frames: int32 [16, 6], replicated, may hold values from -1 to 15, as said below
Outputs:
- branch_out: bfloat16 [16, 1024, 5120], P('batch', 'frame')
The draws below stay inside these ranges and needn't reach their ends.
Inputs may be any that keep to these rules, and one draw needn't show every extreme that they name: `kv_frames`: row f lists frame f in its first slot; its non-negative entries are distinct frames; -1 marks an empty slot, and empty slots follow the listed ones; every row lists 3 or more frames.
All inputs are finite; a program needn't handle non-finite values.
Results may differ from the reference program's by a relative error of at most 0.012.
Values may be sent and summed in bfloat16 or wider, within the bound.
No kernel may reach another device: no remote copies, remote signals or barrier semaphores. Data moves between devices by JAX's collectives and lax.ppermute only.
A program may use at most 128 MiB of HBM per device.

```python
import math
import jax
import jax.numpy as jnp
from jax import lax

D = 5120
HEADS = 40
HEAD_DIM = 128
FRAME_TOKENS = 64
KV_SLOTS = 6
FRAMES = 16
TOKENS = 1024
BATCH = 16


def shared_keys(key):
    base = jnp.clip(jax.random.normal(jax.random.fold_in(key, 11), (BATCH, TOKENS, D), jnp.float32), -6.0, 6.0)
    return base


def draw_keys(key, part):
    base = shared_keys(key)
    return base.astype(jnp.bfloat16)


def draw_queries(key, part):
    key = jax.random.fold_in(key, 1)
    own_draw = jnp.clip(jax.random.normal(key, (BATCH, TOKENS, D), jnp.float32), -6.0, 6.0)
    return own_draw.astype(jnp.bfloat16)


def draw_kv_frames(key, part):
    key = jax.random.fold_in(key, 5)
    row_frame = jnp.arange(FRAMES, dtype=jnp.int32)[:, None]
    col_frame = jnp.arange(FRAMES, dtype=jnp.int32)[None, :]
    noise = jax.random.randint(jax.random.fold_in(key, 1), (FRAMES, FRAMES), 0, 1 << 20)
    priority = noise * FRAMES + col_frame
    priority = priority + jnp.where(row_frame == col_frame, 1 << 29, 0)
    priority = priority + jnp.where(jnp.abs(row_frame - col_frame) == 1, 1 << 28, 0)
    ranked = jnp.argsort(-priority, axis=1, stable=True)[:, :KV_SLOTS].astype(jnp.int32)
    counts = jax.random.randint(jax.random.fold_in(key, 2), (FRAMES, 1), 3, KV_SLOTS + 1)
    counts = jnp.where(row_frame == 0, 3, counts)
    slot_ids = jnp.arange(KV_SLOTS, dtype=jnp.int32)[None, :]
    return jnp.where(slot_ids < counts, ranked, -1).astype(jnp.int32)


def shard_levels(own_key, dims, split, least, top_value):
    factor_of, own = 1.0, jax.random.fold_in(own_key, 6)
    for dim, blocks in split:
        heights = jnp.exp(jax.random.uniform(jax.random.fold_in(own, dim), (blocks,), jnp.float32, least / len(split), top_value / len(split)))
        factor_of = factor_of * jnp.repeat(heights, dims[dim] // blocks).reshape([-1 if axis == dim else 1 for axis in range(len(dims))])
    return factor_of


def normal_values(stream_key, extent, deviation, most, split=(), kind=jnp.bfloat16):
    loudness = shard_levels(stream_key, extent, split, -0.22, 0.18) if split else 1.0
    values = jax.random.normal(stream_key, extent, jnp.float32) * deviation * loudness
    return jnp.minimum(jnp.maximum(values, -most), most).astype(kind)


def setup_inputs(seed: int = 0) -> dict:
    key_of = jax.random.split(jax.random.key(seed), 7)
    return {
        "queries": draw_queries(jax.random.fold_in(key_of[6], 71), 0),
        "keys": draw_keys(jax.random.fold_in(key_of[6], 71), 0),
        "values": normal_values(key_of[2], (BATCH, TOKENS, D), 4.0, 24.0, ((0, 16), (1, 8))),
        "out_weight": normal_values(key_of[3], (D, D), D ** -0.5, 0.078125, ((1, 16),)),
        "gate": normal_values(key_of[4], (BATCH, D), 1.5, 6.0, ((0, 16),), jnp.float32),
        "kv_frames": draw_kv_frames(jax.random.fold_in(key_of[6], 71), 0),
    }


def reference(queries, keys, values, out_weight, gate, kv_frames):
    frame_ids = jnp.arange(FRAMES, dtype=jnp.int32)
    allowed = jnp.any(kv_frames[:, :, None] == frame_ids[None, None, :], axis=1)
    token_mask = jnp.repeat(jnp.repeat(allowed, FRAME_TOKENS, axis=0), FRAME_TOKENS, axis=1)
    score_scale = 1.0 / math.sqrt(HEAD_DIM)

    def one_head(operands):
        query_h, key_h, value_h = operands
        scores = jnp.dot(query_h, key_h.T, preferred_element_type=jnp.float32) * score_scale
        scores = jnp.where(token_mask, scores, -1e+30)
        row_max = lax.optimization_barrier(jnp.max(scores, axis=1, keepdims=True))
        probs = jnp.where(token_mask, jnp.exp(scores - row_max), 0.0)
        denom = lax.optimization_barrier(jnp.sum(probs, axis=1, keepdims=True))
        accum = jnp.dot(probs.astype(jnp.bfloat16), value_h, preferred_element_type=jnp.float32)
        return (accum / denom).astype(jnp.bfloat16)

    def by_heads(array):
        return array.reshape(TOKENS, HEADS, HEAD_DIM).transpose(1, 0, 2)

    def one_prompt(operands):
        query_p, key_p, value_p = operands
        head_outs = lax.map(one_head, (by_heads(query_p), by_heads(key_p), by_heads(value_p)))
        attended = head_outs.transpose(1, 0, 2).reshape(TOKENS, D)
        return jnp.dot(attended, out_weight, preferred_element_type=jnp.float32).astype(jnp.bfloat16)
    projected = lax.map(one_prompt, (queries, keys, values))
    return (gate[:, None, :] * projected.astype(jnp.float32)).astype(jnp.bfloat16)
```

```python
import functools
import math

import jax
import jax.numpy as jnp
from jax import lax
from jax.experimental import pallas as pl
from jax.experimental.pallas import tpu as pltpu
from jax.sharding import Mesh
from jax.sharding import PartitionSpec as P

HEAD_DIM = 128
FRAME = 64
VMEM = 40 * 1024 * 1024


def attend_kernel(meta, q_ref, k_ref, v_ref, o_ref, *, slots, heads):
    frame = meta[0] + pl.program_id(0)
    base = 1 + frame * slots
    lane = lax.broadcasted_iota(jnp.int32, (1, slots * FRAME), 1)
    bias = jnp.zeros((1, slots * FRAME), jnp.float32)
    picks = []
    for s in range(slots):
        g = meta[base + s]
        inside = (lane >= s * FRAME) & (lane < (s + 1) * FRAME)
        bias = jnp.where(inside, jnp.where(g >= 0, 0.0, -1e30), bias)
        g = jnp.maximum(g, 0)
        picks.append((g // 2, pl.multiple_of((g % 2) * FRAME, FRAME)))
    scale = 1.0 / math.sqrt(HEAD_DIM)
    for h in range(heads):
        cols = slice(h * HEAD_DIM, (h + 1) * HEAD_DIM)
        key = jnp.concatenate([k_ref[b, pl.ds(r, FRAME), cols] for b, r in picks], 0)
        val = jnp.concatenate([v_ref[b, pl.ds(r, FRAME), cols] for b, r in picks], 0)
        scores = lax.dot_general(
            q_ref[:, cols], key, (((1,), (1,)), ((), ())), preferred_element_type=jnp.float32
        )
        scores = scores * scale + bias
        top = jnp.max(scores, axis=1, keepdims=True)
        probs = jnp.exp(scores - top)
        denom = jnp.sum(probs, axis=1, keepdims=True)
        accum = jnp.dot(probs.astype(jnp.bfloat16), val, preferred_element_type=jnp.float32)
        o_ref[:, cols] = (accum / denom).astype(jnp.bfloat16)


def attend(meta, parts, frames, slots):
    blocks, _, rows, width = parts.shape
    per = rows // FRAME
    whole = lambda which: pl.BlockSpec(
        (blocks, None, rows, width), lambda i, m: (0, which, 0, 0)
    )
    return pl.pallas_call(
        functools.partial(attend_kernel, slots=slots, heads=width // HEAD_DIM),
        grid_spec=pltpu.PrefetchScalarGridSpec(
            num_scalar_prefetch=1,
            grid=(frames,),
            in_specs=[
                pl.BlockSpec(
                    (None, None, FRAME, width),
                    lambda i, m: ((m[0] + i) // per, 0, (m[0] + i) % per, 0),
                ),
                whole(1),
                whole(2),
            ],
            out_specs=pl.BlockSpec((FRAME, width), lambda i, m: (i, 0)),
        ),
        out_shape=jax.ShapeDtypeStruct((frames * FRAME, width), jnp.bfloat16),
        compiler_params=pltpu.CompilerParams(vmem_limit_bytes=VMEM),
        cost_estimate=pl.CostEstimate(
            flops=frames * FRAME * slots * FRAME * width * 4,
            bytes_accessed=3 * blocks * rows * width * 2,
            transcendentals=frames * FRAME * slots * FRAME * width // HEAD_DIM,
        ),
    )(meta, parts, parts, parts)


def project_kernel(meta, a_ref, b_ref, wa_ref, wb_ref, o_ref):
    nt = (((1,), (1,)), ((), ()))
    total = lax.dot_general(a_ref[...], wa_ref[...], nt, preferred_element_type=jnp.float32)
    total += lax.dot_general(b_ref[...], wb_ref[...], nt, preferred_element_type=jnp.float32)
    o_ref[...] = total.astype(jnp.bfloat16)


def project(meta, mine, other, weight_t, tile=512):
    rows, depth = mine.shape
    width = weight_t.shape[0]
    return pl.pallas_call(
        project_kernel,
        grid_spec=pltpu.PrefetchScalarGridSpec(
            num_scalar_prefetch=1,
            grid=(width // tile,),
            in_specs=[
                pl.BlockSpec((rows, depth), lambda i, m: (0, 0)),
                pl.BlockSpec((rows, depth), lambda i, m: (0, 0)),
                pl.BlockSpec((tile, depth), lambda i, m: (i, m[0])),
                pl.BlockSpec((tile, depth), lambda i, m: (i, 1 - m[0])),
            ],
            out_specs=pl.BlockSpec((rows, tile), lambda i, m: (0, i)),
        ),
        out_shape=jax.ShapeDtypeStruct((rows, width), jnp.bfloat16),
        compiler_params=pltpu.CompilerParams(vmem_limit_bytes=VMEM),
        cost_estimate=pl.CostEstimate(
            flops=4 * rows * depth * width,
            bytes_accessed=4 * depth * width + 2 * rows * width,
            transcendentals=0,
        ),
    )(meta, mine, other, weight_t, weight_t)


def local(queries, keys, values, out_weight, gate, kv_frames):
    rows, width = queries.shape[1:]
    n_y, n_z = lax.axis_size("yh"), lax.axis_size("z")
    n = n_y * n_z
    cols = width // n
    frames, slots = kv_frames.shape
    half = frames // n_y
    my_y, my_z = lax.axis_index("yh"), lax.axis_index("z")

    weight = lax.dynamic_slice_in_dim(out_weight, my_z * (n_y * cols), n_y * cols, 0).T
    weight_t = lax.all_gather(weight, ("x", "yl", "c"), axis=0, tiled=True)

    def blocks(array):
        return array[0].reshape(rows, n_z, n_y, cols).transpose(2, 1, 0, 3).reshape(n, rows, cols)

    parts = jnp.stack([blocks(queries), blocks(keys), blocks(values)], 1)
    parts = lax.all_to_all(parts, ("yh", "z"), 0, 0, tiled=True)

    table = kv_frames.reshape(-1)
    first = lambda y: jnp.concatenate([(y * half)[None].astype(jnp.int32), table])
    theirs = attend(first(1 - my_y), parts, half, slots)
    other = lax.ppermute(theirs, "yh", [(i, 1 - i) for i in range(n_y)])
    mine = attend(first(my_y), parts, half, slots)

    partial = project(my_y[None].astype(jnp.int32), mine, other, weight_t)
    total = lax.psum_scatter(partial, "z", scatter_dimension=0, tiled=True)
    return (gate[:, None, :] * total[None].astype(jnp.float32)).astype(jnp.bfloat16)


def solution(mesh):
    fine = Mesh(mesh.devices.reshape(2, 4, 4, 2, 2), ("yh", "z", "x", "yl", "c"))
    frame, batch = ("yh", "z"), ("x", "yl", "c")
    act = P(batch, frame, None)
    return jax.shard_map(
        local,
        mesh=fine,
        in_specs=(act, act, act, P(None, batch), P(batch, None), P()),
        out_specs=act,
        check_vma=False,
    )
```

```python
import functools
import math

import jax
import jax.numpy as jnp
from jax import lax
from jax.experimental import pallas as pl
from jax.experimental.pallas import tpu as pltpu
from jax.sharding import Mesh
from jax.sharding import PartitionSpec as P

HEAD_DIM = 128
FRAME = 64
VMEM = 60 * 1024 * 1024
NT = (((1,), (1,)), ((), ()))


def params():
    return pltpu.CompilerParams(vmem_limit_bytes=VMEM)


def layout_kernel(q_ref, k_ref, v_ref, o_ref):
    n_y, _, rows, cols = o_ref.shape
    for y in range(n_y):
        for i, ref in enumerate((q_ref, k_ref, v_ref)):
            o_ref[y, i] = ref[:, y * cols : (y + 1) * cols]


def layout(q, k, v, n_y, n_z):
    rows, width = q.shape
    cols = width // (n_y * n_z)
    block = pl.BlockSpec((rows, n_y * cols), lambda i: (0, i))
    return pl.pallas_call(
        layout_kernel,
        grid=(n_z,),
        in_specs=[block] * 3,
        out_specs=pl.BlockSpec((n_y, None, 3, rows, cols), lambda i: (0, i, 0, 0, 0)),
        out_shape=jax.ShapeDtypeStruct((n_y, n_z, 3, rows, cols), q.dtype),
        compiler_params=params(),
        cost_estimate=pl.CostEstimate(flops=0, bytes_accessed=12 * rows * width, transcendentals=0),
    )(q, k, v)


def attend_kernel(meta, q_ref, k_ref, v_ref, o_ref, *, slots):
    blocks, rows, width = q_ref.shape
    per = rows // FRAME
    heads = width // HEAD_DIM
    n_key = slots * FRAME
    scale = 1.0 / math.sqrt(HEAD_DIM)
    lane = lax.broadcasted_iota(jnp.int32, (1, n_key), 1)
    work = []
    for r in range(blocks):
        block = lax.rem(meta[1] + r, blocks)
        for p in range(per):
            base = 2 + ((meta[0] * blocks + block) * per + p) * slots
            bias = jnp.zeros((1, n_key), jnp.float32)
            picks = []
            for s in range(slots):
                g = meta[base + s]
                inside = (lane >= s * FRAME) & (lane < (s + 1) * FRAME)
                bias = jnp.where(inside, jnp.where(g >= 0, 0.0, -1e30), bias)
                g = jnp.maximum(g, 0)
                picks.append((g // per, pl.multiple_of((g % per) * FRAME, FRAME)))
            for h in range(heads):
                work.append((r, p, slice(h * HEAD_DIM, (h + 1) * HEAD_DIM), block, picks, bias))
    scores = []
    for r, p, cols, block, picks, bias in work:
        key = jnp.concatenate([k_ref[b, pl.ds(o, FRAME), cols] for b, o in picks], 0)
        query = q_ref[block, p * FRAME : (p + 1) * FRAME, cols]
        score = lax.dot_general(query, key, NT, preferred_element_type=jnp.float32)
        scores.append(score * scale + bias)
    tops = [jnp.max(s, axis=1, keepdims=True) for s in scores]
    probs = [jnp.exp(s - t) for s, t in zip(scores, tops)]
    denoms = [jnp.sum(p, axis=1, keepdims=True) for p in probs]
    for (r, p, cols, block, picks, bias), prob, denom in zip(work, probs, denoms):
        val = jnp.concatenate([v_ref[b, pl.ds(o, FRAME), cols] for b, o in picks], 0)
        accum = jnp.dot(prob.astype(jnp.bfloat16), val, preferred_element_type=jnp.float32)
        o_ref[r, p * FRAME : (p + 1) * FRAME, cols] = (accum / denom).astype(jnp.bfloat16)


def attend(meta, parts, slots, n_y):
    blocks, _, rows, width = parts.shape
    n_z = blocks // n_y
    whole = lambda which: pl.BlockSpec((blocks, None, rows, width), lambda i, m: (0, which, 0, 0))
    work = n_z * rows * slots * FRAME * width
    return pl.pallas_call(
        functools.partial(attend_kernel, slots=slots),
        grid_spec=pltpu.PrefetchScalarGridSpec(
            num_scalar_prefetch=1,
            grid=(1,),
            in_specs=[
                pl.BlockSpec((n_z, None, rows, width), lambda i, m: (m[0], 0, 0, 0)),
                whole(1),
                whole(2),
            ],
            out_specs=pl.BlockSpec((n_z, rows, width), lambda i, m: (0, 0, 0)),
        ),
        out_shape=jax.ShapeDtypeStruct((n_z, rows, width), jnp.bfloat16),
        compiler_params=params(),
        cost_estimate=pl.CostEstimate(
            flops=work * 4, bytes_accessed=3 * blocks * rows * width * 2, transcendentals=work // HEAD_DIM
        ),
    )(meta, parts, parts, parts)


def project_kernel(meta, a_ref, b_ref, w_ref, o0, o1a, o1b, o2a, o2b, o3a, o3b):
    n_z, rows, depth = a_ref.shape
    flat = (n_z * rows, depth)
    step = pl.program_id(0)
    here = pl.ds(pl.multiple_of(meta[0] * depth, 128), depth)
    there = pl.ds(pl.multiple_of((1 - meta[0]) * depth, 128), depth)
    total = lax.dot_general(a_ref[...].reshape(flat), w_ref[:, here], NT, preferred_element_type=jnp.float32)
    total += lax.dot_general(b_ref[...].reshape(flat), w_ref[:, there], NT, preferred_element_type=jnp.float32)
    total = total.astype(jnp.bfloat16)
    o0[...] = total[:rows]

    @pl.when(step == 0)
    def _():
        o1a[...] = total[rows : 2 * rows]
        o2a[...] = total[2 * rows : 3 * rows]
        o3a[...] = total[3 * rows :]

    @pl.when(step == 1)
    def _():
        o1b[...] = total[rows : 2 * rows]
        o2b[...] = total[2 * rows : 3 * rows]
        o3b[...] = total[3 * rows :]


def project(meta, mine, other, weight_t):
    n_z, rows, depth = mine.shape
    width = weight_t.shape[0]
    tile = width // 2
    act = pl.BlockSpec((n_z, rows, depth), lambda i, m: (0, 0, 0))
    part = pl.BlockSpec((rows, tile), lambda i, m: (0, 0))
    return pl.pallas_call(
        project_kernel,
        grid_spec=pltpu.PrefetchScalarGridSpec(
            num_scalar_prefetch=1,
            grid=(2,),
            in_specs=[act, act, pl.BlockSpec((tile, 2 * depth), lambda i, m: (i, 0))],
            out_specs=[pl.BlockSpec((rows, tile), lambda i, m: (0, i))] + [part] * 6,
        ),
        out_shape=[jax.ShapeDtypeStruct((rows, width), jnp.bfloat16)]
        + [jax.ShapeDtypeStruct((rows, tile), jnp.bfloat16)] * 6,
        compiler_params=params(),
        cost_estimate=pl.CostEstimate(
            flops=4 * n_z * rows * depth * width,
            bytes_accessed=4 * depth * width + 2 * n_z * rows * width,
            transcendentals=0,
        ),
    )(meta, mine, other, weight_t)


def add_kernel(a_ref, b_ref, o_ref):
    o_ref[...] = (a_ref[...].astype(jnp.float32) + b_ref[...].astype(jnp.float32)).astype(o_ref.dtype)


def add(a, b):
    return pl.pallas_call(
        add_kernel,
        out_shape=jax.ShapeDtypeStruct(a.shape, a.dtype),
        compiler_params=params(),
        cost_estimate=pl.CostEstimate(flops=a.size, bytes_accessed=6 * a.size, transcendentals=0),
    )(a, b)


def finish_kernel(meta, gate_ref, *refs):
    o_ref = refs[-1]
    width = o_ref.shape[2] // 2
    early = pl.program_id(0) < pl.num_programs(0) // 2
    for part in range(2):
        own, low_a, low_b, high_a, high_b = (r[...].astype(jnp.float32) for r in refs[5 * part : 5 * part + 5])
        total = own + jnp.where(early, low_a, low_b) + jnp.where(early, high_a, high_b)
        total = total.astype(jnp.bfloat16).astype(jnp.float32)
        y = meta[0] if part == 0 else 1 - meta[0]
        cols = pl.ds(pl.multiple_of(y * width, 128), width)
        o_ref[0, :, cols] = (gate_ref[:, cols] * total).astype(o_ref.dtype)


def finish(meta, gate, parts):
    rows, width = parts[0][0].shape
    steps = 4
    tile = width // steps
    half = [pl.BlockSpec((rows, tile), lambda i, m: (0, jnp.minimum(i, steps // 2 - 1)))]
    half += [pl.BlockSpec((rows, tile), lambda i, m: (0, jnp.maximum(i - steps // 2, 0)))]
    args, specs = [], []
    for own, low, high in parts:
        args += [own, *low, *high]
        specs += [pl.BlockSpec((rows, tile), lambda i, m: (0, i))] + half + half
    return pl.pallas_call(
        finish_kernel,
        grid_spec=pltpu.PrefetchScalarGridSpec(
            num_scalar_prefetch=1,
            grid=(steps,),
            in_specs=[pl.BlockSpec((1, 2 * tile), lambda i, m: (0, i))] + specs,
            out_specs=pl.BlockSpec((1, rows, 2 * tile), lambda i, m: (0, 0, i)),
        ),
        out_shape=jax.ShapeDtypeStruct((1, rows, 2 * width), jnp.bfloat16),
        compiler_params=params(),
    )(meta, gate, *args)


def local(queries, keys, values, out_weight, gate, kv_frames):
    rows, width = queries.shape[1:]
    n_y, n_z = lax.axis_size("yh"), lax.axis_size("z")
    n_l = lax.axis_size("yl")
    n = n_y * n_z
    cols = width // n
    slots = kv_frames.shape[1]
    my_y, my_z, my_l = (lax.axis_index(a).astype(jnp.int32) for a in ("yh", "z", "yl"))

    def shift(array, axes, size, by):
        return lax.ppermute(array, axes, [(i, (i + by) % size) for i in range(size)])

    parts = layout(queries[0], keys[0], values[0], n_y, n_z).reshape(n, 3, rows, cols)
    parts = lax.all_to_all(parts, ("yh", "z"), 0, 0, tiled=True)

    weight = lax.dynamic_slice_in_dim(out_weight, my_z * (n_y * cols), n_y * cols, 0).T
    split = weight.shape[0] // 2
    ring = n_y * n_l
    far = jnp.concatenate(
        [shift(weight[:split], ("yh", "yl"), ring, 1), shift(weight[split:], ("yh", "yl"), ring, ring - 1)], 0
    )
    weight_near = lax.all_gather(weight, ("x", "c"), axis=0, tiled=True)
    weight_far = lax.all_gather(far, ("x", "c"), axis=0, tiled=True)

    table = kv_frames.reshape(-1)
    meta = lambda y: jnp.concatenate([jnp.stack([y, my_z]), table])
    theirs = attend(meta(1 - my_y), parts, slots, n_y)
    other = shift(theirs, "yh", n_y, 1)
    mine = attend(meta(my_y), parts, slots, n_y)

    up = lambda array: shift(array, "z", n_z, 1)
    down = lambda array: shift(array, "z", n_z, n_z - 1)
    sums = []
    for piece in (weight_near, weight_far):
        o0, o1a, o1b, o2a, o2b, o3a, o3b = project(my_y[None], mine, other, piece)
        relay_a, relay_b = up(o2a), down(o2b)
        low_b, high_a = up(o1b), down(o3a)
        low_a, high_b = up(add(o1a, relay_a)), down(add(o3b, relay_b))
        sums.append((o0, (low_a, low_b), (high_a, high_b)))
    return finish(my_l[None], gate, sums)


def solution(mesh):
    fine = Mesh(mesh.devices.reshape(2, 4, 4, 2, 2), ("yh", "z", "x", "yl", "c"))
    frame, batch = ("yh", "z"), ("x", "yl", "c")
    act = P(batch, frame, None)
    return jax.shard_map(
        local,
        mesh=fine,
        in_specs=(act, act, act, P(None, batch), P(batch, None), P()),
        out_specs=act,
        check_vma=False,
    )
```

```python
import functools
import math

import jax
import jax.numpy as jnp
from jax import lax
from jax.experimental import pallas as pl
from jax.experimental.pallas import tpu as pltpu
from jax.sharding import Mesh
from jax.sharding import PartitionSpec as P

HEAD_DIM = 128
FRAME = 64
VMEM = 60 * 1024 * 1024
NT = (((1,), (1,)), ((), ()))


def params():
    return pltpu.CompilerParams(vmem_limit_bytes=VMEM)


def layout_kernel(q_ref, k_ref, v_ref, o_ref):
    n_y, _, rows, cols = o_ref.shape
    for y in range(n_y):
        for i, ref in enumerate((q_ref, k_ref, v_ref)):
            o_ref[y, i] = ref[:, y * cols : (y + 1) * cols]


def layout(q, k, v, n_y, n_z):
    rows, width = q.shape
    cols = width // (n_y * n_z)
    block = pl.BlockSpec((rows, n_y * cols), lambda i: (0, i))
    return pl.pallas_call(
        layout_kernel,
        grid=(n_z,),
        in_specs=[block] * 3,
        out_specs=pl.BlockSpec((n_y, None, 3, rows, cols), lambda i: (0, i, 0, 0, 0)),
        out_shape=jax.ShapeDtypeStruct((n_y, n_z, 3, rows, cols), q.dtype),
        compiler_params=params(),
        cost_estimate=pl.CostEstimate(flops=0, bytes_accessed=12 * rows * width, transcendentals=0),
    )(q, k, v)


def attend_kernel(meta, q_ref, k_ref, v_ref, o_ref, *, slots):
    blocks, rows, width = q_ref.shape
    per = rows // FRAME
    heads = width // HEAD_DIM
    n_key = slots * FRAME
    scale = 1.0 / math.sqrt(HEAD_DIM)
    lane = lax.broadcasted_iota(jnp.int32, (1, n_key), 1)
    work = []
    for r in range(blocks):
        block = lax.rem(meta[1] + r, blocks)
        for p in range(per):
            base = 2 + ((meta[0] * blocks + block) * per + p) * slots
            bias = jnp.zeros((1, n_key), jnp.float32)
            picks = []
            for s in range(slots):
                g = meta[base + s]
                inside = (lane >= s * FRAME) & (lane < (s + 1) * FRAME)
                bias = jnp.where(inside, jnp.where(g >= 0, 0.0, -1e30), bias)
                g = jnp.maximum(g, 0)
                picks.append((g // per, pl.multiple_of((g % per) * FRAME, FRAME)))
            for h in range(heads):
                work.append((r, p, slice(h * HEAD_DIM, (h + 1) * HEAD_DIM), block, picks, bias))
    scores = []
    for r, p, cols, block, picks, bias in work:
        key = jnp.concatenate([k_ref[b, pl.ds(o, FRAME), cols] for b, o in picks], 0)
        query = q_ref[block, p * FRAME : (p + 1) * FRAME, cols]
        score = lax.dot_general(query, key, NT, preferred_element_type=jnp.float32)
        scores.append(score * scale + bias)
    tops = [jnp.max(s, axis=1, keepdims=True) for s in scores]
    probs = [jnp.exp(s - t) for s, t in zip(scores, tops)]
    denoms = [jnp.sum(p, axis=1, keepdims=True) for p in probs]
    for (r, p, cols, block, picks, bias), prob, denom in zip(work, probs, denoms):
        val = jnp.concatenate([v_ref[b, pl.ds(o, FRAME), cols] for b, o in picks], 0)
        accum = jnp.dot(prob.astype(jnp.bfloat16), val, preferred_element_type=jnp.float32)
        o_ref[r, p * FRAME : (p + 1) * FRAME, cols] = (accum / denom).astype(jnp.bfloat16)


def attend(meta, parts, slots, n_y):
    blocks, _, rows, width = parts.shape
    n_z = blocks // n_y
    whole = lambda which: pl.BlockSpec((blocks, None, rows, width), lambda i, m: (0, which, 0, 0))
    work = n_z * rows * slots * FRAME * width
    return pl.pallas_call(
        functools.partial(attend_kernel, slots=slots),
        grid_spec=pltpu.PrefetchScalarGridSpec(
            num_scalar_prefetch=1,
            grid=(1,),
            in_specs=[
                pl.BlockSpec((n_z, None, rows, width), lambda i, m: (m[0], 0, 0, 0)),
                whole(1),
                whole(2),
            ],
            out_specs=pl.BlockSpec((n_z, rows, width), lambda i, m: (0, 0, 0)),
        ),
        out_shape=jax.ShapeDtypeStruct((n_z, rows, width), jnp.bfloat16),
        compiler_params=params(),
        cost_estimate=pl.CostEstimate(
            flops=work * 4, bytes_accessed=3 * blocks * rows * width * 2, transcendentals=work // HEAD_DIM
        ),
    )(meta, parts, parts, parts)


def own_kernel(meta, a_ref, w_ref, o_ref):
    n_z, rows, depth = a_ref.shape
    act = a_ref[...].reshape(n_z * rows, depth)
    o_ref[...] = lax.dot_general(act, w_ref[...], NT, preferred_element_type=jnp.float32)


def project_own(meta, mine, weight_t, tile=640):
    n_z, rows, depth = mine.shape
    width = weight_t.shape[0]
    return pl.pallas_call(
        own_kernel,
        grid_spec=pltpu.PrefetchScalarGridSpec(
            num_scalar_prefetch=1,
            grid=(width // tile,),
            in_specs=[
                pl.BlockSpec((n_z, rows, depth), lambda i, m: (0, 0, 0)),
                pl.BlockSpec((tile, depth), lambda i, m: (i, m[0])),
            ],
            out_specs=pl.BlockSpec((n_z * rows, tile), lambda i, m: (0, i)),
        ),
        out_shape=jax.ShapeDtypeStruct((n_z * rows, width), jnp.float32),
        compiler_params=params(),
        cost_estimate=pl.CostEstimate(
            flops=2 * n_z * rows * depth * width,
            bytes_accessed=2 * depth * width + 4 * n_z * rows * width,
            transcendentals=0,
        ),
    )(meta, mine, weight_t)


def project_kernel(meta, *refs, with_own):
    if with_own:
        base_ref, a_ref, w_ref, stay, up, down, up_late, down_late = refs
    else:
        m_ref, a_ref, w_ref, stay, up, down, up_late, down_late, act = refs
    n_z, rows, depth = a_ref.shape
    flat = (n_z * rows, depth)
    step, half = pl.program_id(0), pl.num_programs(0) // 2
    if with_own:
        total = base_ref[...] + lax.dot_general(
            a_ref[...].reshape(flat), w_ref[...], NT, preferred_element_type=jnp.float32
        )
    else:

        @pl.when(step == 0)
        def _():
            act[:, pl.ds(pl.multiple_of(meta[0] * depth, 128), depth)] = m_ref[...].reshape(flat)
            act[:, pl.ds(pl.multiple_of((1 - meta[0]) * depth, 128), depth)] = a_ref[...].reshape(flat)

        total = lax.dot_general(act[...], w_ref[...], NT, preferred_element_type=jnp.float32)
    total = total.astype(jnp.bfloat16)
    stay[...] = total[:rows]
    tile = total.shape[1]
    cols = pl.ds(pl.multiple_of(lax.rem(step, half) * tile, 128), tile)

    @pl.when(step < half)
    def _():
        up[0, :, cols] = total[2 * rows : 3 * rows]
        down[1, :, cols] = total[3 * rows :]
        up_late[...] = total[rows : 2 * rows]

    @pl.when(step >= half)
    def _():
        up[1, :, cols] = total[rows : 2 * rows]
        down[0, :, cols] = total[2 * rows : 3 * rows]
        down_late[...] = total[3 * rows :]


def project(meta, own, other, weight_t, tile=640):
    n_z, rows, depth = other.shape
    width = weight_t.shape[0]
    with_own = own.ndim == 2
    steps = width // tile
    half = steps // 2
    act = pl.BlockSpec((n_z, rows, depth), lambda i, m: (0, 0, 0))
    first = lambda i: jnp.minimum(i, half - 1)
    second = lambda i: jnp.maximum(i - half, 0)
    if with_own:
        in_specs = [
            pl.BlockSpec((n_z * rows, tile), lambda i, m: (0, i)),
            act,
            pl.BlockSpec((tile, depth), lambda i, m: (i, 1 - m[0])),
        ]
        scratch = []
    else:
        in_specs = [act, act, pl.BlockSpec((tile, 2 * depth), lambda i, m: (i, 0))]
        scratch = [pltpu.VMEM((n_z * rows, 2 * depth), jnp.bfloat16)]
    pair = pl.BlockSpec((2, rows, width // 2), lambda i, m: (0, 0, 0))
    return pl.pallas_call(
        functools.partial(project_kernel, with_own=with_own),
        grid_spec=pltpu.PrefetchScalarGridSpec(
            num_scalar_prefetch=1,
            grid=(steps,),
            in_specs=in_specs,
            out_specs=[
                pl.BlockSpec((rows, tile), lambda i, m: (0, i)),
                pair,
                pair,
                pl.BlockSpec((rows, tile), lambda i, m: (0, first(i))),
                pl.BlockSpec((rows, tile), lambda i, m: (0, second(i))),
            ],
            scratch_shapes=scratch,
        ),
        out_shape=[
            jax.ShapeDtypeStruct((rows, width), jnp.bfloat16),
            jax.ShapeDtypeStruct((2, rows, width // 2), jnp.bfloat16),
            jax.ShapeDtypeStruct((2, rows, width // 2), jnp.bfloat16),
            jax.ShapeDtypeStruct((rows, width // 2), jnp.bfloat16),
            jax.ShapeDtypeStruct((rows, width // 2), jnp.bfloat16),
        ],
        compiler_params=params(),
        cost_estimate=pl.CostEstimate(
            flops=4 * n_z * rows * depth * width,
            bytes_accessed=4 * depth * width + 2 * n_z * rows * width,
            transcendentals=0,
        ),
    )(meta, own, other, weight_t)


def add_kernel(a_ref, x_ref, b_ref, y_ref, oa_ref, ob_ref):
    wide = lambda ref: ref[...].astype(jnp.float32)
    oa_ref[...] = (wide(a_ref) + wide(x_ref)).astype(oa_ref.dtype)
    ob_ref[...] = (wide(b_ref) + wide(y_ref)).astype(ob_ref.dtype)


def add_relayed(a, from_low, b, from_high, steps=2):
    rows, width = a.shape
    tile = width // steps
    flat = pl.BlockSpec((rows, tile), lambda i: (0, i))
    lead = pl.BlockSpec((None, rows, tile), lambda i: (0, 0, i))
    return pl.pallas_call(
        add_kernel,
        grid=(steps,),
        in_specs=[flat, lead, flat, lead],
        out_specs=[flat, flat],
        out_shape=[jax.ShapeDtypeStruct(a.shape, a.dtype)] * 2,
        compiler_params=params(),
        cost_estimate=pl.CostEstimate(flops=2 * a.size, bytes_accessed=12 * a.size, transcendentals=0),
    )(a, from_low, b, from_high)


def finish_kernel(meta, gate_ref, own, low_b, low_a, high_a, high_b, *refs):
    o_ref = refs[-1]
    early = pl.program_id(0) < pl.num_programs(0) // 2
    wide = lambda ref: ref[...].astype(jnp.float32)
    total = wide(own) + jnp.where(early, wide(low_a), wide(low_b)) + jnp.where(early, wide(high_a), wide(high_b))
    total = total.astype(jnp.bfloat16).astype(jnp.float32)
    o_ref[0] = (gate_ref[...] * total).astype(o_ref.dtype)


def finish(meta, gate, piece, out=None):
    own, low, low_a, high, high_b = piece
    rows, width = own.shape
    steps = 4
    tile = width // steps
    half = steps // 2
    first = lambda i: jnp.minimum(i, half - 1)
    second = lambda i: jnp.maximum(i - half, 0)
    specs = [
        pl.BlockSpec((1, tile), lambda i, m: (0, 2 * i + m[0])),
        pl.BlockSpec((rows, tile), lambda i, m: (0, i)),
        pl.BlockSpec((None, rows, tile), lambda i, m: (1, 0, second(i))),
        pl.BlockSpec((rows, tile), lambda i, m: (0, first(i))),
        pl.BlockSpec((None, rows, tile), lambda i, m: (1, 0, first(i))),
        pl.BlockSpec((rows, tile), lambda i, m: (0, second(i))),
    ]
    args = [meta, gate, own, low, low_a, high, high_b]
    alias = {}
    if out is not None:
        alias = {len(args): 0}
        args.append(out)
        specs.append(pl.BlockSpec(memory_space=pl.ANY))
    return pl.pallas_call(
        finish_kernel,
        grid_spec=pltpu.PrefetchScalarGridSpec(
            num_scalar_prefetch=1,
            grid=(steps,),
            in_specs=specs,
            out_specs=pl.BlockSpec((1, rows, tile), lambda i, m: (0, 0, 2 * i + m[0])),
        ),
        out_shape=jax.ShapeDtypeStruct((1, rows, 2 * width), jnp.bfloat16),
        input_output_aliases=alias,
        compiler_params=params(),
        cost_estimate=pl.CostEstimate(flops=4 * rows * width, bytes_accessed=8 * rows * width, transcendentals=0),
    )(*args)


def local(queries, keys, values, out_weight, gate, kv_frames):
    rows, width = queries.shape[1:]
    n_y, n_z = lax.axis_size("yh"), lax.axis_size("z")
    n_l = lax.axis_size("yl")
    n = n_y * n_z
    cols = width // n
    slots = kv_frames.shape[1]
    my_y, my_z, my_l = (lax.axis_index(a).astype(jnp.int32) for a in ("yh", "z", "yl"))

    def shift(array, axes, size, by):
        return lax.ppermute(array, axes, [(i, (i + by) % size) for i in range(size)])

    weight = lax.dynamic_slice_in_dim(out_weight, my_z * (n_y * cols), n_y * cols, 0)
    split = weight.shape[1] // 2
    ring = n_y * n_l
    lower, upper = weight[:, :split].T, weight[:, split:].T
    lower, upper, queries = lax.optimization_barrier((lower, upper, queries))
    far = shift(lower, ("yh", "yl"), ring, 1), shift(upper, ("yh", "yl"), ring, ring - 1)
    weight_near = lax.all_gather(jnp.concatenate([lower, upper], 0), ("x", "c"), axis=0, tiled=True)

    parts = layout(queries[0], keys[0], values[0], n_y, n_z).reshape(n, 3, rows, cols)
    parts, *far = lax.optimization_barrier((parts, *far))
    weight_far = lax.all_gather(jnp.concatenate(far, 0), ("x", "c"), axis=0, tiled=True)
    parts = lax.all_to_all(parts, ("yh", "z"), 0, 0, tiled=True)

    table = kv_frames.reshape(-1)
    meta = lambda y: jnp.concatenate([jnp.stack([y, my_z]), table])
    theirs = attend(meta(1 - my_y), parts, slots, n_y)
    other = shift(theirs, "yh", n_y, 1)
    mine = attend(meta(my_y), parts, slots, n_y)

    up = lambda array: shift(array, "z", n_z, 1)
    down = lambda array: shift(array, "z", n_z, n_z - 1)

    def scatter(own, weight_t):
        stay, to_high, to_low, late_high, late_low = project(my_y[None], own, other, weight_t)
        low, high = up(to_high), down(to_low)
        late_high, late_low = add_relayed(late_high, low, late_low, high)
        return stay, low, up(late_high), high, down(late_low)

    near = scatter(project_own(my_y[None], mine, weight_near), weight_near)
    far = scatter(mine, weight_far)
    out = finish(my_l[None], gate, near)
    return finish(1 - my_l[None], gate, far, out)


def solution(mesh):
    fine = Mesh(mesh.devices.reshape(2, 4, 4, 2, 2), ("yh", "z", "x", "yl", "c"))
    frame, batch = ("yh", "z"), ("x", "yl", "c")
    act = P(batch, frame, None)
    return jax.shard_map(
        local,
        mesh=fine,
        in_specs=(act, act, act, P(None, batch), P(batch, None), P()),
        out_specs=act,
        check_vma=False,
    )
```

```python
import functools
import math

import jax
import jax.numpy as jnp
from jax import lax
from jax.experimental import pallas as pl
from jax.experimental.pallas import tpu as pltpu
from jax.sharding import Mesh
from jax.sharding import PartitionSpec as P

HEAD_DIM = 128
FRAME = 64
MIB = 1024 * 1024
VMEM = 60 * MIB
NT = (((1,), (1,)), ((), ()))


def params(limit=VMEM):
    return pltpu.CompilerParams(vmem_limit_bytes=limit)


def layout_kernel(q_ref, k_ref, v_ref, o_ref):
    n_y, _, rows, cols = o_ref.shape
    for y in range(n_y):
        for i, ref in enumerate((q_ref, k_ref, v_ref)):
            o_ref[y, i] = ref[:, y * cols : (y + 1) * cols]


def layout(q, k, v, n_y, n_z):
    rows, width = q.shape
    cols = width // (n_y * n_z)
    block = pl.BlockSpec((rows, n_y * cols), lambda i: (0, i))
    return pl.pallas_call(
        layout_kernel,
        grid=(n_z,),
        in_specs=[block] * 3,
        out_specs=pl.BlockSpec((n_y, None, 3, rows, cols), lambda i: (0, i, 0, 0, 0)),
        out_shape=jax.ShapeDtypeStruct((n_y, n_z, 3, rows, cols), q.dtype),
        compiler_params=params(),
        cost_estimate=pl.CostEstimate(flops=0, bytes_accessed=12 * rows * width, transcendentals=0),
    )(q, k, v)


def attend_half(meta, half, q_ref, k_ref, v_ref, o_ref, slots):
    blocks, rows, width = o_ref.shape
    per = rows // FRAME
    heads = width // HEAD_DIM
    n_key = slots * FRAME
    scale = 1.0 / math.sqrt(HEAD_DIM)
    lane = lax.broadcasted_iota(jnp.int32, (1, n_key), 1)
    work = []
    for r in range(blocks):
        block = half * blocks + lax.rem(meta[1] + r, blocks)
        for p in range(per):
            base = 2 + (block * per + p) * slots
            bias = jnp.zeros((1, n_key), jnp.float32)
            picks = []
            for s in range(slots):
                g = meta[base + s]
                inside = (lane >= s * FRAME) & (lane < (s + 1) * FRAME)
                bias = jnp.where(inside, jnp.where(g >= 0, 0.0, -1e30), bias)
                g = jnp.maximum(g, 0)
                picks.append((g // per, pl.multiple_of((g % per) * FRAME, FRAME)))
            for h in range(heads):
                work.append((r, p, slice(h * HEAD_DIM, (h + 1) * HEAD_DIM), block, picks, bias))
    scores = []
    for r, p, cols, block, picks, bias in work:
        key = jnp.concatenate([k_ref[b, pl.ds(o, FRAME), cols] for b, o in picks], 0)
        query = q_ref[block, p * FRAME : (p + 1) * FRAME, cols]
        score = lax.dot_general(query, key, NT, preferred_element_type=jnp.float32)
        scores.append(score * scale + bias)
    tops = [jnp.max(s, axis=1, keepdims=True) for s in scores]
    probs = [jnp.exp(s - t) for s, t in zip(scores, tops)]
    denoms = [jnp.sum(p, axis=1, keepdims=True) for p in probs]
    for (r, p, cols, block, picks, bias), prob, denom in zip(work, probs, denoms):
        val = jnp.concatenate([v_ref[b, pl.ds(o, FRAME), cols] for b, o in picks], 0)
        accum = jnp.dot(prob.astype(jnp.bfloat16), val, preferred_element_type=jnp.float32)
        o_ref[r, p * FRAME : (p + 1) * FRAME, cols] = (accum / denom).astype(jnp.bfloat16)


def attend_kernel(meta, q_ref, k_ref, v_ref, theirs_ref, mine_ref, *, slots):
    attend_half(meta, 1 - meta[0], q_ref, k_ref, v_ref, theirs_ref, slots)
    attend_half(meta, meta[0], q_ref, k_ref, v_ref, mine_ref, slots)


def attend(meta, parts, slots, n_y):
    blocks, _, rows, width = parts.shape
    n_z = blocks // n_y
    whole = lambda which: pl.BlockSpec((blocks, None, rows, width), lambda i, m: (0, which, 0, 0))
    work = blocks * rows * slots * FRAME * width
    return pl.pallas_call(
        functools.partial(attend_kernel, slots=slots),
        grid_spec=pltpu.PrefetchScalarGridSpec(
            num_scalar_prefetch=1,
            grid=(1,),
            in_specs=[whole(0), whole(1), whole(2)],
            out_specs=[pl.BlockSpec((n_z, rows, width), lambda i, m: (0, 0, 0))] * 2,
        ),
        out_shape=[jax.ShapeDtypeStruct((n_z, rows, width), jnp.bfloat16)] * 2,
        compiler_params=params(),
        cost_estimate=pl.CostEstimate(
            flops=work * 4, bytes_accessed=4 * blocks * rows * width * 2, transcendentals=work // HEAD_DIM
        ),
    )(meta, parts, parts, parts)


def project_kernel(meta, mine_ref, other_ref, *refs, spots, n_piece):
    n_x = len(spots)
    pieces, refs = refs[:n_piece], refs[n_piece:]
    outs, (act, w_buf, r_buf, a_sem, w_sem, r_sem) = refs[:5], refs[5:]
    n_z, rows, depth = mine_ref.shape
    tile = w_buf.shape[0] // n_x
    part = tile // 4
    half, core = meta[0], meta[1]
    loads = {}

    def load(x):
        copies = []
        for k in range(4):
            buffer, row = spots[x][k % 2]
            src = pieces[buffer + k // 2 * (n_piece // 2)].at[pl.ds(row, part)]
            row = x * tile + ((core if k < 2 else 1 - core) * 2 + k % 2) * part
            dst = w_buf.at[pl.ds(pl.multiple_of(row, part), part)]
            copies.append(pltpu.make_async_copy(src, dst, w_sem.at[4 * x + k]))
        for copy in copies:
            copy.start()
        loads[x] = copies

    acts = []
    for i, (ref, at) in enumerate(((mine_ref, half), (other_ref, 1 - half))):
        cols = pl.ds(pl.multiple_of(at * depth, 128), depth)
        acts.append(pltpu.make_async_copy(ref, act.at[:, :, cols], a_sem.at[i]))
        acts[-1].start()
    load(0)
    load(1)
    for copy in acts:
        copy.wait()

    stores = []
    for x in range(n_x):
        for copy in loads[x]:
            copy.wait()
        if x + 2 < n_x:
            load(x + 2)
        left = act[...].reshape(n_z * rows, 2 * depth)
        weight = w_buf[x * tile : (x + 1) * tile]
        total = lax.dot_general(left, weight, NT, preferred_element_type=jnp.float32)
        r_buf[x] = total.astype(r_buf.dtype)
        stay, up, down, up_late, down_late = outs
        late, col = divmod(x, n_x // 2)
        block = lambda r: r_buf.at[x, pl.ds(r * rows, rows)]
        cols = pl.ds(col * tile, tile)
        targets = [(block(0), stay.at[:, pl.ds(x * tile, tile)])]
        if late:
            targets += [(block(1), up.at[1, :, cols]), (block(2), down.at[0, :, cols]), (block(3), down_late.at[:, cols])]
        else:
            targets += [(block(2), up.at[0, :, cols]), (block(3), down.at[1, :, cols]), (block(1), up_late.at[:, cols])]
        for src, dst in targets:
            copy = pltpu.make_async_copy(src, dst, r_sem.at[len(stores)])
            copy.start()
            stores.append(copy)
    for copy in stores:
        copy.wait()


def project(meta, mine, other, pieces, spots, part):
    n_z, rows, depth = mine.shape
    n_x = len(spots)
    tile = 4 * part
    width = n_x * tile
    shape = lambda *dims: jax.ShapeDtypeStruct(dims, jnp.bfloat16)
    hbm = pl.BlockSpec(memory_space=pl.ANY)
    return pl.pallas_call(
        functools.partial(project_kernel, spots=spots, n_piece=len(pieces)),
        grid_spec=pltpu.PrefetchScalarGridSpec(
            num_scalar_prefetch=1,
            grid=(1,),
            in_specs=[hbm] * (2 + len(pieces)),
            out_specs=[hbm] * 5,
            scratch_shapes=[
                pltpu.VMEM((n_z, rows, 2 * depth), jnp.bfloat16),
                pltpu.VMEM((width, 2 * depth), jnp.bfloat16),
                pltpu.VMEM((n_x, n_z * rows, tile), jnp.bfloat16),
                pltpu.SemaphoreType.DMA((2,)),
                pltpu.SemaphoreType.DMA((4 * n_x,)),
                pltpu.SemaphoreType.DMA((n_x * n_z,)),
            ],
        ),
        out_shape=[shape(rows, width)] + [shape(2, rows, width // 2)] * 2 + [shape(rows, width // 2)] * 2,
        compiler_params=params(),
        cost_estimate=pl.CostEstimate(
            flops=4 * n_z * rows * depth * width,
            bytes_accessed=4 * depth * width + 4 * n_z * rows * width,
            transcendentals=0,
        ),
    )(meta, mine, other, *pieces)


def add_kernel(a_ref, x_ref, b_ref, y_ref, oa_ref, ob_ref):
    wide = lambda ref: ref[...].astype(jnp.float32)
    oa_ref[...] = (wide(a_ref) + wide(x_ref)).astype(oa_ref.dtype)
    ob_ref[...] = (wide(b_ref) + wide(y_ref)).astype(ob_ref.dtype)


def add_relayed(a, from_low, b, from_high, steps=2):
    rows, width = a.shape
    tile = width // steps
    flat = pl.BlockSpec((rows, tile), lambda i: (0, i))
    lead = pl.BlockSpec((None, rows, tile), lambda i: (0, 0, i))
    return pl.pallas_call(
        add_kernel,
        grid=(steps,),
        in_specs=[flat, lead, flat, lead],
        out_specs=[flat, flat],
        out_shape=[jax.ShapeDtypeStruct(a.shape, a.dtype)] * 2,
        compiler_params=params(8 * MIB),
        cost_estimate=pl.CostEstimate(flops=2 * a.size, bytes_accessed=12 * a.size, transcendentals=0),
    )(a, from_low, b, from_high)


def finish_kernel(meta, gate_ref, own, low_b, low_a, high_a, high_b, *refs):
    o_ref = refs[-1]
    early = pl.program_id(0) < pl.num_programs(0) // 2
    wide = lambda ref: ref[...].astype(jnp.float32)
    total = wide(own) + jnp.where(early, wide(low_a), wide(low_b)) + jnp.where(early, wide(high_a), wide(high_b))
    total = total.astype(jnp.bfloat16).astype(jnp.float32)
    o_ref[0] = (gate_ref[...] * total).astype(o_ref.dtype)


def finish(meta, gate, piece, out=None):
    own, low, low_a, high, high_b = piece
    rows, width = own.shape
    steps = 4
    tile = width // steps
    half = steps // 2
    first = lambda i: jnp.minimum(i, half - 1)
    second = lambda i: jnp.maximum(i - half, 0)
    place = lambda i, m: 2 * lax.rem(m[1] + i, steps) + m[0]
    specs = [
        pl.BlockSpec((1, tile), lambda i, m: (0, place(i, m))),
        pl.BlockSpec((rows, tile), lambda i, m: (0, i)),
        pl.BlockSpec((None, rows, tile), lambda i, m: (1, 0, second(i))),
        pl.BlockSpec((rows, tile), lambda i, m: (0, first(i))),
        pl.BlockSpec((None, rows, tile), lambda i, m: (1, 0, first(i))),
        pl.BlockSpec((rows, tile), lambda i, m: (0, second(i))),
    ]
    args = [meta, gate, own, low, low_a, high, high_b]
    alias = {}
    if out is not None:
        alias = {len(args): 0}
        args.append(out)
        specs.append(pl.BlockSpec(memory_space=pl.ANY))
    return pl.pallas_call(
        finish_kernel,
        grid_spec=pltpu.PrefetchScalarGridSpec(
            num_scalar_prefetch=1,
            grid=(steps,),
            in_specs=specs,
            out_specs=pl.BlockSpec((1, rows, tile), lambda i, m: (0, 0, place(i, m))),
        ),
        out_shape=jax.ShapeDtypeStruct((1, rows, 2 * width), jnp.bfloat16),
        input_output_aliases=alias,
        compiler_params=params(12 * MIB),
        cost_estimate=pl.CostEstimate(flops=4 * rows * width, bytes_accessed=8 * rows * width, transcendentals=0),
    )(*args)


def local(queries, keys, values, out_weight, gate, kv_frames):
    rows, width = queries.shape[1:]
    n_y, n_z, n_l = lax.axis_size("yh"), lax.axis_size("z"), lax.axis_size("yl")
    n = n_y * n_z
    cols = width // n
    slots = kv_frames.shape[1]
    axes = ("yh", "z", "x", "yl", "c")
    my_y, my_z, my_x, my_l, my_c = (lax.axis_index(a).astype(jnp.int32) for a in axes)
    after = lax.optimization_barrier

    def shift(array, axes, size, by):
        return lax.ppermute(array, axes, [(i, (i + by) % size) for i in range(size)])

    up = lambda array: shift(array, "z", n_z, 1)
    down = lambda array: shift(array, "z", n_z, n_z - 1)
    swap = lambda array: shift(array, "c", 2, 1)

    weight = lax.dynamic_slice_in_dim(out_weight, my_z * (n_y * cols), n_y * cols, 0)
    part = weight.shape[1] // 2
    ring, n_x = n_y * n_l, lax.axis_size("x")
    right = lambda *arrays: shift(jnp.concatenate(arrays, 0), "x", n_x, 1)
    left = lambda *arrays: shift(jnp.concatenate(arrays, 0), "x", n_x, n_x - 1)
    lower, upper = weight[:, :part].T, weight[:, part:].T
    lower, upper, queries = after((lower, upper, queries))
    far_l, far_u = shift(lower, ("yh", "yl"), ring, 1), shift(upper, ("yh", "yl"), ring, ring - 1)
    near_l, near_u = right(lower), left(upper)
    parts = layout(queries[0], keys[0], values[0], n_y, n_z).reshape(n, 3, rows, cols)
    parts, far_l, far_u, near_l, near_u = after((parts, far_l, far_u, near_l, near_u))
    parts = lax.all_to_all(parts, ("yh", "z"), 0, 0, tiled=True)
    held = jnp.concatenate([lower, upper, near_l, near_u, far_l, far_u], 0)
    low, high = right(upper, near_l, far_l), left(lower, near_u, far_u)
    near = [held, low, high]
    near = near + [swap(piece) for piece in near]
    far = [right(far_u, low[2 * part :]), left(far_l, high[2 * part :])]
    rows_of = lambda *spots: [(buffer, row * part) for buffer, row in spots]
    near_spots = [rows_of(*pair) for pair in (((0, 0), (0, 1)), ((2, 0), (0, 3)), ((1, 1), (2, 1)), ((0, 2), (1, 0)))]
    far_spots = [rows_of(*pair) for pair in (((0, 4), (0, 5)), ((4, 0), (2, 2)), ((3, 1), (4, 1)), ((1, 2), (3, 0)))]

    table = kv_frames.reshape(-1)
    meta = jnp.concatenate([jnp.stack([my_y, my_z]), table])
    parts, near = after((parts, near))
    theirs, mine = attend(meta, parts, slots, n_y)
    other = shift(theirs, "yh", n_y, 1)

    def relay(sent):
        stay, to_up, to_down, late_up, late_down = sent
        return stay, up(to_up), down(to_down), late_up, late_down

    def last(relayed):
        stay, low, high, late_up, late_down = relayed
        late_up, late_down = add_relayed(late_up, low, late_down, high)
        return stay, low, up(late_up), high, down(late_down)

    here = jnp.stack([my_y, my_c])
    other, far = after((other, far))
    far = near[:3] + far + near[3:] + [swap(piece) for piece in far]
    sent = relay(project(here, mine, other, near, near_spots, part))
    sent_far = relay(project(here, mine, other, far, far_spots, part))
    out = finish(jnp.stack([my_l, my_x]), gate, last(sent))
    return finish(jnp.stack([1 - my_l, my_x]), gate, last(sent_far), out)


def solution(mesh):
    fine = Mesh(mesh.devices.reshape(2, 4, 4, 2, 2), ("yh", "z", "x", "yl", "c"))
    frame, batch = ("yh", "z"), ("x", "yl", "c")
    act = P(batch, frame, None)
    return jax.shard_map(
        local,
        mesh=fine,
        in_specs=(act, act, act, P(None, batch), P(batch, None), P()),
        out_specs=act,
        check_vma=False,
    )
```

```python
import functools
import math

import jax
import jax.numpy as jnp
from jax import lax
from jax.experimental import pallas as pl
from jax.experimental.pallas import tpu as pltpu
from jax.sharding import Mesh
from jax.sharding import PartitionSpec as P

HEAD_DIM = 128
FRAME = 64
MIB = 1024 * 1024
VMEM = 60 * MIB
NT = (((1,), (1,)), ((), ()))


def params(limit=VMEM):
    return pltpu.CompilerParams(vmem_limit_bytes=limit)


def layout_kernel(q_ref, k_ref, v_ref, o_ref):
    n_y, _, rows, cols = o_ref.shape
    for y in range(n_y):
        for i, ref in enumerate((q_ref, k_ref, v_ref)):
            o_ref[y, i] = ref[:, y * cols : (y + 1) * cols]


def layout(q, k, v, n_y, n_z):
    rows, width = q.shape
    cols = width // (n_y * n_z)
    block = pl.BlockSpec((rows, n_y * cols), lambda i: (0, i))
    return pl.pallas_call(
        layout_kernel,
        grid=(n_z,),
        in_specs=[block] * 3,
        out_specs=pl.BlockSpec((n_y, None, 3, rows, cols), lambda i: (0, i, 0, 0, 0)),
        out_shape=jax.ShapeDtypeStruct((n_y, n_z, 3, rows, cols), q.dtype),
        compiler_params=params(8 * MIB),
        cost_estimate=pl.CostEstimate(flops=0, bytes_accessed=12 * rows * width, transcendentals=0),
    )(q, k, v)


def attend_kernel(meta, q_ref, k_ref, v_ref, o_ref, *, slots):
    blocks, rows, width = q_ref.shape
    per = rows // FRAME
    heads = width // HEAD_DIM
    n_key = slots * FRAME
    scale = 1.0 / math.sqrt(HEAD_DIM)
    lane = lax.broadcasted_iota(jnp.int32, (1, n_key), 1)
    work = []
    for r in range(blocks):
        block = lax.rem(meta[1] + r, blocks)
        for p in range(per):
            base = 2 + ((meta[0] * blocks + block) * per + p) * slots
            bias = jnp.zeros((1, n_key), jnp.float32)
            picks = []
            for s in range(slots):
                g = meta[base + s]
                inside = (lane >= s * FRAME) & (lane < (s + 1) * FRAME)
                bias = jnp.where(inside, jnp.where(g >= 0, 0.0, -1e30), bias)
                g = jnp.maximum(g, 0)
                picks.append((g // per, pl.multiple_of((g % per) * FRAME, FRAME)))
            for h in range(heads):
                work.append((r, p, slice(h * HEAD_DIM, (h + 1) * HEAD_DIM), block, picks, bias))
    scores = []
    for r, p, cols, block, picks, bias in work:
        key = jnp.concatenate([k_ref[b, pl.ds(o, FRAME), cols] for b, o in picks], 0)
        query = q_ref[block, p * FRAME : (p + 1) * FRAME, cols]
        score = lax.dot_general(query, key, NT, preferred_element_type=jnp.float32)
        scores.append(score * scale + bias)
    tops = [jnp.max(s, axis=1, keepdims=True) for s in scores]
    probs = [jnp.exp(s - t) for s, t in zip(scores, tops)]
    denoms = [jnp.sum(p, axis=1, keepdims=True) for p in probs]
    for (r, p, cols, block, picks, bias), prob, denom in zip(work, probs, denoms):
        val = jnp.concatenate([v_ref[b, pl.ds(o, FRAME), cols] for b, o in picks], 0)
        accum = jnp.dot(prob.astype(jnp.bfloat16), val, preferred_element_type=jnp.float32)
        o_ref[r, p * FRAME : (p + 1) * FRAME, cols] = (accum / denom).astype(jnp.bfloat16)


def attend(meta, parts, slots, n_y):
    blocks, _, rows, width = parts.shape
    n_z = blocks // n_y
    whole = lambda which: pl.BlockSpec((blocks, None, rows, width), lambda i, m: (0, which, 0, 0))
    work = n_z * rows * slots * FRAME * width
    return pl.pallas_call(
        functools.partial(attend_kernel, slots=slots),
        grid_spec=pltpu.PrefetchScalarGridSpec(
            num_scalar_prefetch=1,
            grid=(1,),
            in_specs=[
                pl.BlockSpec((n_z, None, rows, width), lambda i, m: (m[0], 0, 0, 0)),
                whole(1),
                whole(2),
            ],
            out_specs=pl.BlockSpec((n_z, rows, width), lambda i, m: (0, 0, 0)),
        ),
        out_shape=jax.ShapeDtypeStruct((n_z, rows, width), jnp.bfloat16),
        compiler_params=params(32 * MIB),
        cost_estimate=pl.CostEstimate(
            flops=work * 4, bytes_accessed=3 * blocks * rows * width * 2, transcendentals=work // HEAD_DIM
        ),
    )(meta, parts, parts, parts)


def project_kernel(meta, mine_ref, other_ref, *refs, spots, n_piece, paired):
    n_x = len(spots)
    pieces, refs = refs[:n_piece], refs[n_piece:]
    outs, (act, w_buf, r_buf, a_sem, w_sem, r_sem) = refs[:-6], refs[-6:]
    if paired:
        stay, up, down, up_late, down_late = outs
        up, up_next, down, down_next = up.at[0], up.at[1], down.at[0], down.at[1]
    else:
        stay, up, up_next, down, down_next, up_late, down_late = outs
    n_z, rows, depth = mine_ref.shape
    tile = w_buf.shape[0] // n_x
    part = tile // 4
    half, core = meta[0], meta[1]
    loads = {}

    def load(x):
        copies = []
        for k in range(4):
            buffer, row = spots[x][k % 2]
            src = pieces[buffer + k // 2 * (n_piece // 2)].at[pl.ds(row, part)]
            row = x * tile + ((core if k < 2 else 1 - core) * 2 + k % 2) * part
            dst = w_buf.at[pl.ds(pl.multiple_of(row, part), part)]
            copies.append(pltpu.make_async_copy(src, dst, w_sem.at[4 * x + k]))
        for copy in copies:
            copy.start()
        loads[x] = copies

    acts = []
    for i, (ref, at) in enumerate(((mine_ref, half), (other_ref, 1 - half))):
        cols = pl.ds(pl.multiple_of(at * depth, 128), depth)
        acts.append(pltpu.make_async_copy(ref, act.at[:, :, cols], a_sem.at[i]))
        acts[-1].start()
    load(0)
    load(1)
    for copy in acts:
        copy.wait()

    stores = []
    for x in range(n_x):
        for copy in loads[x]:
            copy.wait()
        if x + 2 < n_x:
            load(x + 2)
        left = act[...].reshape(n_z * rows, 2 * depth)
        weight = w_buf[x * tile : (x + 1) * tile]
        total = lax.dot_general(left, weight, NT, preferred_element_type=jnp.float32)
        r_buf[x] = total.astype(r_buf.dtype)
        late, col = divmod(x, n_x // 2)
        block = lambda r: r_buf.at[x, pl.ds(r * rows, rows)]
        cols = pl.ds(col * tile, tile)
        targets = [(block(0), stay.at[:, pl.ds(x * tile, tile)])]
        if late:
            there = (up_next, down, down_late)
        else:
            there = (up_late, up, down_next)
        targets += [(block(r + 1), ref.at[:, cols]) for r, ref in enumerate(there)]
        for src, dst in targets:
            copy = pltpu.make_async_copy(src, dst, r_sem.at[len(stores)])
            copy.start()
            stores.append(copy)
    for copy in stores:
        copy.wait()


def project(meta, mine, other, pieces, spots, part, paired):
    n_z, rows, depth = mine.shape
    n_x = len(spots)
    tile = 4 * part
    width = n_x * tile
    shape = lambda *dims: jax.ShapeDtypeStruct(dims, jnp.bfloat16)
    half = shape(rows, width // 2)
    sent = [shape(2, rows, width // 2)] * 2 if paired else [half] * 4
    hbm = pl.BlockSpec(memory_space=pl.ANY)
    return pl.pallas_call(
        functools.partial(project_kernel, spots=spots, n_piece=len(pieces), paired=paired),
        grid_spec=pltpu.PrefetchScalarGridSpec(
            num_scalar_prefetch=1,
            grid=(1,),
            in_specs=[hbm] * (2 + len(pieces)),
            out_specs=[hbm] * (3 + len(sent)),
            scratch_shapes=[
                pltpu.VMEM((n_z, rows, 2 * depth), jnp.bfloat16),
                pltpu.VMEM((width, 2 * depth), jnp.bfloat16),
                pltpu.VMEM((n_x, n_z * rows, tile), jnp.bfloat16),
                pltpu.SemaphoreType.DMA((2,)),
                pltpu.SemaphoreType.DMA((4 * n_x,)),
                pltpu.SemaphoreType.DMA((n_x * n_z,)),
            ],
        ),
        out_shape=[shape(rows, width), *sent, half, half],
        compiler_params=params(16 * MIB if paired else VMEM),
        cost_estimate=pl.CostEstimate(
            flops=4 * n_z * rows * depth * width,
            bytes_accessed=4 * depth * width + 4 * n_z * rows * width,
            transcendentals=0,
        ),
    )(meta, mine, other, *pieces)


def add_kernel(a_ref, x_ref, b_ref, y_ref, oa_ref, ob_ref):
    wide = lambda ref: ref[...].astype(jnp.float32)
    oa_ref[...] = (wide(a_ref) + wide(x_ref)).astype(oa_ref.dtype)
    ob_ref[...] = (wide(b_ref) + wide(y_ref)).astype(ob_ref.dtype)


def add_relayed(a, from_low, b, from_high):
    rows, width = a.shape
    flat = pl.BlockSpec((rows, width), lambda i: (0, 0))
    lead = pl.BlockSpec((None, rows, width), lambda i: (0, 0, 0))
    got = lead if from_low.ndim == 3 else flat
    return pl.pallas_call(
        add_kernel,
        grid=(1,),
        in_specs=[flat, got, flat, got],
        out_specs=[flat, flat],
        out_shape=[jax.ShapeDtypeStruct(a.shape, a.dtype)] * 2,
        compiler_params=params(4 * MIB),
        cost_estimate=pl.CostEstimate(flops=2 * a.size, bytes_accessed=12 * a.size, transcendentals=0),
    )(a, from_low, b, from_high)


def finish_kernel(meta, gate_ref, own, low_b, low_a, high_a, high_b, *refs):
    o_ref, buf, sem = refs[-3:]
    n_x, _, tile = buf.shape
    half = n_x // 2
    wide = lambda value: value.astype(jnp.float32)
    whole = lambda ref: ref[1] if len(ref.shape) == 3 else ref[...]
    low, high = (whole(low_a), whole(low_b)), (whole(high_a), whole(high_b))
    copies = []
    for x in range(n_x):
        late, at = divmod(x, half)
        cols = slice(at * tile, (at + 1) * tile)
        total = wide(own[:, x * tile : (x + 1) * tile]) + wide(low[late][:, cols]) + wide(high[late][:, cols])
        total = total.astype(jnp.bfloat16).astype(jnp.float32)
        place = pl.ds(pl.multiple_of((2 * lax.rem(meta[1] + x, n_x) + meta[0]) * tile, 128), tile)
        buf[x] = (gate_ref[:, place] * total).astype(buf.dtype)
        copies.append(pltpu.make_async_copy(buf.at[x], o_ref.at[0, :, place], sem.at[x]))
        copies[-1].start()
    for copy in copies:
        copy.wait()


def finish(meta, gate, piece, out=None):
    rows, width = piece[0].shape
    n_x = 4
    hbm = pl.BlockSpec(memory_space=pl.ANY)
    whole = lambda array: pl.BlockSpec(array.shape, lambda i, m: (0,) * array.ndim)
    args, specs = [gate, *piece], [whole(array) for array in (gate, *piece)]
    alias = {}
    if out is not None:
        alias = {len(args) + 1: 0}
        args.append(out)
        specs.append(hbm)
    return pl.pallas_call(
        finish_kernel,
        grid_spec=pltpu.PrefetchScalarGridSpec(
            num_scalar_prefetch=1,
            grid=(1,),
            in_specs=specs,
            out_specs=hbm,
            scratch_shapes=[pltpu.VMEM((n_x, rows, width // n_x), jnp.bfloat16), pltpu.SemaphoreType.DMA((n_x,))],
        ),
        out_shape=jax.ShapeDtypeStruct((1, rows, 2 * width), jnp.bfloat16),
        input_output_aliases=alias,
        compiler_params=params(8 * MIB),
        cost_estimate=pl.CostEstimate(flops=4 * rows * width, bytes_accessed=8 * rows * width, transcendentals=0),
    )(meta, *args)


def local(queries, keys, values, out_weight, gate, kv_frames):
    rows, width = queries.shape[1:]
    n_y, n_z, n_l = lax.axis_size("yh"), lax.axis_size("z"), lax.axis_size("yl")
    n = n_y * n_z
    cols = width // n
    slots = kv_frames.shape[1]
    axes = ("yh", "z", "x", "yl", "c")
    my_y, my_z, my_x, my_l, my_c = (lax.axis_index(a).astype(jnp.int32) for a in axes)
    after = lax.optimization_barrier

    def shift(array, axes, size, by):
        return lax.ppermute(array, axes, [(i, (i + by) % size) for i in range(size)])

    up = lambda array: shift(array, "z", n_z, 1)
    down = lambda array: shift(array, "z", n_z, n_z - 1)
    swap = lambda array: shift(array, "c", 2, 1)

    weight = lax.dynamic_slice_in_dim(out_weight, my_z * (n_y * cols), n_y * cols, 0)
    part = weight.shape[1] // 2
    ring, n_x = n_y * n_l, lax.axis_size("x")
    right = lambda *arrays: shift(jnp.concatenate(arrays, 0), "x", n_x, 1)
    left = lambda *arrays: shift(jnp.concatenate(arrays, 0), "x", n_x, n_x - 1)
    lower, upper = weight[:, :part].T, weight[:, part:].T
    lower, upper, queries = after((lower, upper, queries))
    far_l, far_u = shift(lower, ("yh", "yl"), ring, 1), shift(upper, ("yh", "yl"), ring, ring - 1)
    parts = layout(queries[0], keys[0], values[0], n_y, n_z).reshape(n, 3, rows, cols)
    parts, lower, upper = after((parts, lower, upper))
    near_l, near_u = right(lower), left(upper)
    parts, far_l, far_u = after((parts, far_l, far_u))
    parts = lax.all_to_all(parts, ("yh", "z"), 0, 0, tiled=True)
    held = jnp.concatenate([lower, upper, near_l, near_u, far_l, far_u], 0)
    low, high = right(upper, near_l, far_l), left(lower, near_u, far_u)
    near = [held, low, high]
    near = near + [swap(piece) for piece in near]
    far = [right(far_u, low[2 * part :]), left(far_l, high[2 * part :])]
    rows_of = lambda *spots: [(buffer, row * part) for buffer, row in spots]
    near_spots = [rows_of(*pair) for pair in (((0, 0), (0, 1)), ((2, 0), (0, 3)), ((1, 1), (2, 1)), ((0, 2), (1, 0)))]
    far_spots = [rows_of(*pair) for pair in (((0, 4), (0, 5)), ((4, 0), (2, 2)), ((3, 1), (4, 1)), ((1, 2), (3, 0)))]

    table = kv_frames.reshape(-1)
    meta = lambda y: jnp.concatenate([jnp.stack([y, my_z]), table])
    parts, near = after((parts, near))
    theirs = attend(meta(1 - my_y), parts, slots, n_y)
    other = shift(theirs, "yh", n_y, 1)
    mine = attend(meta(my_y), parts, slots, n_y)

    def relay(sent):
        if len(sent) == 5:
            stay, to_up, to_down, late_up, late_down = sent
            low, high = up(to_up), down(to_down)
            return stay, low, low, high, high, late_up, late_down
        stay, to_up, next_up, to_down, next_down, late_up, late_down = sent
        return stay, up(to_up), up(next_up), down(to_down), down(next_down), late_up, late_down

    def last(relayed):
        stay, low, low_b, high, high_a, late_up, late_down = relayed
        late_up, late_down = add_relayed(late_up, low, late_down, high)
        return stay, low_b, up(late_up), high_a, down(late_down)

    here = jnp.stack([my_y, my_c])
    sent = project(here, mine, other, near, near_spots, part, True)
    far, sent = after((far, sent))
    far = near[:3] + far + near[3:] + [swap(piece) for piece in far]
    sent = relay(sent)
    sent_far = relay(project(here, mine, other, far, far_spots, part, False))
    out = finish(jnp.stack([my_l, my_x]), gate, last(sent))
    return finish(jnp.stack([1 - my_l, my_x]), gate, last(sent_far), out)


def solution(mesh):
    fine = Mesh(mesh.devices.reshape(2, 4, 4, 2, 2), ("yh", "z", "x", "yl", "c"))
    frame, batch = ("yh", "z"), ("x", "yl", "c")
    act = P(batch, frame, None)
    return jax.shard_map(
        local,
        mesh=fine,
        in_specs=(act, act, act, P(None, batch), P(batch, None), P()),
        out_specs=act,
        check_vma=False,
    )
```

```python
import functools
import math

import jax
import jax.numpy as jnp
from jax import lax
from jax.experimental import pallas as pl
from jax.experimental.pallas import tpu as pltpu
from jax.sharding import Mesh
from jax.sharding import PartitionSpec as P

HEAD_DIM = 128
FRAME = 64
MIB = 1024 * 1024
VMEM = 60 * MIB
NT = (((1,), (1,)), ((), ()))


def params(limit=VMEM):
    return pltpu.CompilerParams(vmem_limit_bytes=limit)


def layout_kernel(q_ref, k_ref, v_ref, o_ref):
    n_y, _, rows, cols = o_ref.shape
    for y in range(n_y):
        for i, ref in enumerate((q_ref, k_ref, v_ref)):
            o_ref[y, i] = ref[:, y * cols : (y + 1) * cols]


def layout(q, k, v, n_y, n_z):
    rows, width = q.shape
    cols = width // (n_y * n_z)
    block = pl.BlockSpec((rows, n_y * cols), lambda i: (0, i))
    return pl.pallas_call(
        layout_kernel,
        grid=(n_z,),
        in_specs=[block] * 3,
        out_specs=pl.BlockSpec((n_y, None, 3, rows, cols), lambda i: (0, i, 0, 0, 0)),
        out_shape=jax.ShapeDtypeStruct((n_y, n_z, 3, rows, cols), q.dtype),
        compiler_params=params(8 * MIB),
        cost_estimate=pl.CostEstimate(flops=0, bytes_accessed=12 * rows * width, transcendentals=0),
    )(q, k, v)


def attend_kernel(meta, q_ref, k_ref, v_ref, o_ref, *, slots):
    blocks, rows, width = q_ref.shape
    per = rows // FRAME
    heads = width // HEAD_DIM
    n_key = slots * FRAME
    scale = 1.0 / math.sqrt(HEAD_DIM)
    lane = lax.broadcasted_iota(jnp.int32, (1, n_key), 1)
    work = []
    for r in range(blocks):
        block = lax.rem(meta[1] + r, blocks)
        for p in range(per):
            base = 2 + ((meta[0] * blocks + block) * per + p) * slots
            bias = jnp.zeros((1, n_key), jnp.float32)
            picks = []
            for s in range(slots):
                g = meta[base + s]
                inside = (lane >= s * FRAME) & (lane < (s + 1) * FRAME)
                bias = jnp.where(inside, jnp.where(g >= 0, 0.0, -1e30), bias)
                g = jnp.maximum(g, 0)
                picks.append((g // per, pl.multiple_of((g % per) * FRAME, FRAME)))
            for h in range(heads):
                work.append((r, p, slice(h * HEAD_DIM, (h + 1) * HEAD_DIM), block, picks, bias))
    scores = []
    for r, p, cols, block, picks, bias in work:
        key = jnp.concatenate([k_ref[b, pl.ds(o, FRAME), cols] for b, o in picks], 0)
        query = q_ref[block, p * FRAME : (p + 1) * FRAME, cols]
        score = lax.dot_general(query, key, NT, preferred_element_type=jnp.float32)
        scores.append(score * scale + bias)
    tops = [jnp.max(s, axis=1, keepdims=True) for s in scores]
    probs = [jnp.exp(s - t) for s, t in zip(scores, tops)]
    denoms = [jnp.sum(p, axis=1, keepdims=True) for p in probs]
    for (r, p, cols, block, picks, bias), prob, denom in zip(work, probs, denoms):
        val = jnp.concatenate([v_ref[b, pl.ds(o, FRAME), cols] for b, o in picks], 0)
        accum = jnp.dot(prob.astype(jnp.bfloat16), val, preferred_element_type=jnp.float32)
        o_ref[r, p * FRAME : (p + 1) * FRAME, cols] = (accum / denom).astype(jnp.bfloat16)


def attend(meta, parts, slots, n_y):
    blocks, _, rows, width = parts.shape
    n_z = blocks // n_y
    whole = lambda which: pl.BlockSpec((blocks, None, rows, width), lambda i, m: (0, which, 0, 0))
    work = n_z * rows * slots * FRAME * width
    return pl.pallas_call(
        functools.partial(attend_kernel, slots=slots),
        grid_spec=pltpu.PrefetchScalarGridSpec(
            num_scalar_prefetch=1,
            grid=(1,),
            in_specs=[
                pl.BlockSpec((n_z, None, rows, width), lambda i, m: (m[0], 0, 0, 0)),
                whole(1),
                whole(2),
            ],
            out_specs=pl.BlockSpec((n_z, rows, width), lambda i, m: (0, 0, 0)),
        ),
        out_shape=jax.ShapeDtypeStruct((n_z, rows, width), jnp.bfloat16),
        compiler_params=params(32 * MIB),
        cost_estimate=pl.CostEstimate(
            flops=work * 4, bytes_accessed=3 * blocks * rows * width * 2, transcendentals=work // HEAD_DIM
        ),
    )(meta, parts, parts, parts)


def project_kernel(meta, mine_ref, other_ref, *refs, spots, n_piece, paired):
    n_x = len(spots)
    pieces, refs = refs[:n_piece], refs[n_piece:]
    outs, (act, w_buf, r_buf, a_sem, w_sem, r_sem) = refs[:-6], refs[-6:]
    if paired:
        stay, up, down, up_late, down_late = outs
        up, up_next, down, down_next = up.at[0], up.at[1], down.at[0], down.at[1]
    else:
        stay, up, up_next, down, down_next, up_late, down_late = outs
    n_z, rows, depth = mine_ref.shape
    tile = w_buf.shape[0] // n_x
    part = tile // 4
    half, core = meta[0], meta[1]
    loads = {}

    def load(x):
        copies = []
        for k in range(4):
            buffer, row = spots[x][k % 2]
            src = pieces[buffer + k // 2 * (n_piece // 2)].at[pl.ds(row, part)]
            row = x * tile + ((core if k < 2 else 1 - core) * 2 + k % 2) * part
            dst = w_buf.at[pl.ds(pl.multiple_of(row, part), part)]
            copies.append(pltpu.make_async_copy(src, dst, w_sem.at[4 * x + k]))
        for copy in copies:
            copy.start()
        loads[x] = copies

    acts = []
    for i, (ref, at) in enumerate(((mine_ref, half), (other_ref, 1 - half))):
        cols = pl.ds(pl.multiple_of(at * depth, 128), depth)
        acts.append(pltpu.make_async_copy(ref, act.at[:, :, cols], a_sem.at[i]))
        acts[-1].start()
    load(0)
    load(1)
    for copy in acts:
        copy.wait()

    stores = []
    for x in range(n_x):
        for copy in loads[x]:
            copy.wait()
        if x + 2 < n_x:
            load(x + 2)
        left = act[...].reshape(n_z * rows, 2 * depth)
        weight = w_buf[x * tile : (x + 1) * tile]
        total = lax.dot_general(left, weight, NT, preferred_element_type=jnp.float32)
        r_buf[x] = total.astype(r_buf.dtype)
        late, col = divmod(x, n_x // 2)
        block = lambda r: r_buf.at[x, pl.ds(r * rows, rows)]
        cols = pl.ds(col * tile, tile)
        targets = [(block(0), stay.at[:, pl.ds(x * tile, tile)])]
        if late:
            there = (up_next, down, down_late)
        else:
            there = (up_late, up, down_next)
        targets += [(block(r + 1), ref.at[:, cols]) for r, ref in enumerate(there)]
        for src, dst in targets:
            copy = pltpu.make_async_copy(src, dst, r_sem.at[len(stores)])
            copy.start()
            stores.append(copy)
    for copy in stores:
        copy.wait()


def project(meta, mine, other, pieces, spots, part, paired):
    n_z, rows, depth = mine.shape
    n_x = len(spots)
    tile = 4 * part
    width = n_x * tile
    shape = lambda *dims: jax.ShapeDtypeStruct(dims, jnp.bfloat16)
    half = shape(rows, width // 2)
    sent = [shape(2, rows, width // 2)] * 2 if paired else [half] * 4
    hbm = pl.BlockSpec(memory_space=pl.ANY)
    return pl.pallas_call(
        functools.partial(project_kernel, spots=spots, n_piece=len(pieces), paired=paired),
        grid_spec=pltpu.PrefetchScalarGridSpec(
            num_scalar_prefetch=1,
            grid=(1,),
            in_specs=[hbm] * (2 + len(pieces)),
            out_specs=[hbm] * (3 + len(sent)),
            scratch_shapes=[
                pltpu.VMEM((n_z, rows, 2 * depth), jnp.bfloat16),
                pltpu.VMEM((width, 2 * depth), jnp.bfloat16),
                pltpu.VMEM((n_x, n_z * rows, tile), jnp.bfloat16),
                pltpu.SemaphoreType.DMA((2,)),
                pltpu.SemaphoreType.DMA((4 * n_x,)),
                pltpu.SemaphoreType.DMA((n_x * n_z,)),
            ],
        ),
        out_shape=[shape(rows, width), *sent, half, half],
        compiler_params=params(16 * MIB),
        cost_estimate=pl.CostEstimate(
            flops=4 * n_z * rows * depth * width,
            bytes_accessed=4 * depth * width + 4 * n_z * rows * width,
            transcendentals=0,
        ),
    )(meta, mine, other, *pieces)


def add_kernel(a_ref, x_ref, b_ref, y_ref, oa_ref, ob_ref):
    wide = lambda ref: ref[...].astype(jnp.float32)
    oa_ref[...] = (wide(a_ref) + wide(x_ref)).astype(oa_ref.dtype)
    ob_ref[...] = (wide(b_ref) + wide(y_ref)).astype(ob_ref.dtype)


def add_relayed(a, from_low, b, from_high):
    rows, width = a.shape
    flat = pl.BlockSpec((rows, width), lambda i: (0, 0))
    lead = pl.BlockSpec((None, rows, width), lambda i: (0, 0, 0))
    got = lead if from_low.ndim == 3 else flat
    return pl.pallas_call(
        add_kernel,
        grid=(1,),
        in_specs=[flat, got, flat, got],
        out_specs=[flat, flat],
        out_shape=[jax.ShapeDtypeStruct(a.shape, a.dtype)] * 2,
        compiler_params=params(4 * MIB),
        cost_estimate=pl.CostEstimate(flops=2 * a.size, bytes_accessed=12 * a.size, transcendentals=0),
    )(a, from_low, b, from_high)


def finish_kernel(meta, gate_ref, own, low_b, low_a, high_a, high_b, *refs):
    o_ref, buf, sem = refs[-3:]
    n_x, _, tile = buf.shape
    half = n_x // 2
    wide = lambda value: value.astype(jnp.float32)
    whole = lambda ref: ref[1] if len(ref.shape) == 3 else ref[...]
    low, high = (whole(low_a), whole(low_b)), (whole(high_a), whole(high_b))
    copies = []
    for x in range(n_x):
        late, at = divmod(x, half)
        cols = slice(at * tile, (at + 1) * tile)
        total = wide(own[:, x * tile : (x + 1) * tile]) + wide(low[late][:, cols]) + wide(high[late][:, cols])
        total = total.astype(jnp.bfloat16).astype(jnp.float32)
        place = pl.ds(pl.multiple_of((2 * lax.rem(meta[1] + x, n_x) + meta[0]) * tile, 128), tile)
        buf[x] = (gate_ref[:, place] * total).astype(buf.dtype)
        copies.append(pltpu.make_async_copy(buf.at[x], o_ref.at[0, :, place], sem.at[x]))
        copies[-1].start()
    for copy in copies:
        copy.wait()


def finish(meta, gate, piece, out=None):
    rows, width = piece[0].shape
    n_x = 4
    hbm = pl.BlockSpec(memory_space=pl.ANY)
    whole = lambda array: pl.BlockSpec(array.shape, lambda i, m: (0,) * array.ndim)
    args, specs = [gate, *piece], [whole(array) for array in (gate, *piece)]
    alias = {}
    if out is not None:
        alias = {len(args) + 1: 0}
        args.append(out)
        specs.append(hbm)
    return pl.pallas_call(
        finish_kernel,
        grid_spec=pltpu.PrefetchScalarGridSpec(
            num_scalar_prefetch=1,
            grid=(1,),
            in_specs=specs,
            out_specs=hbm,
            scratch_shapes=[pltpu.VMEM((n_x, rows, width // n_x), jnp.bfloat16), pltpu.SemaphoreType.DMA((n_x,))],
        ),
        out_shape=jax.ShapeDtypeStruct((1, rows, 2 * width), jnp.bfloat16),
        input_output_aliases=alias,
        compiler_params=params(8 * MIB),
        cost_estimate=pl.CostEstimate(flops=4 * rows * width, bytes_accessed=8 * rows * width, transcendentals=0),
    )(meta, *args)


def local(queries, keys, values, out_weight, gate, kv_frames):
    rows, width = queries.shape[1:]
    n_y, n_z, n_l = lax.axis_size("yh"), lax.axis_size("z"), lax.axis_size("yl")
    n = n_y * n_z
    cols = width // n
    slots = kv_frames.shape[1]
    axes = ("yh", "z", "x", "yl", "c")
    my_y, my_z, my_x, my_l, my_c = (lax.axis_index(a).astype(jnp.int32) for a in axes)
    after = lax.optimization_barrier

    def shift(array, axes, size, by):
        return lax.ppermute(array, axes, [(i, (i + by) % size) for i in range(size)])

    up = lambda array: shift(array, "z", n_z, 1)
    down = lambda array: shift(array, "z", n_z, n_z - 1)
    swap = lambda array: shift(array, "c", 2, 1)

    weight = lax.dynamic_slice_in_dim(out_weight, my_z * (n_y * cols), n_y * cols, 0)
    part = weight.shape[1] // 2
    ring, n_x = n_y * n_l, lax.axis_size("x")
    right = lambda *arrays: shift(jnp.concatenate(arrays, 0), "x", n_x, 1)
    left = lambda *arrays: shift(jnp.concatenate(arrays, 0), "x", n_x, n_x - 1)
    lower, upper = weight[:, :part].T, weight[:, part:].T
    lower, upper, queries = after((lower, upper, queries))
    far_l, far_u = shift(lower, ("yh", "yl"), ring, 1), shift(upper, ("yh", "yl"), ring, ring - 1)
    parts = layout(queries[0], keys[0], values[0], n_y, n_z).reshape(n, 3, rows, cols)
    near_l, near_u = right(lower), left(upper)
    parts, far_l, far_u = after((parts, far_l, far_u))
    parts = lax.all_to_all(parts, ("yh", "z"), 0, 0, tiled=True)
    near_l, near_u, lower, upper = after((near_l, near_u, lower, upper))
    held = jnp.concatenate([lower, upper, near_l, near_u, far_l, far_u], 0)
    low, high = right(upper, near_l, far_l), left(lower, near_u, far_u)
    near = [held, low, high]
    near = near + [swap(piece) for piece in near]
    far = [right(far_u, low[2 * part :]), left(far_l, high[2 * part :])]
    rows_of = lambda *spots: [(buffer, row * part) for buffer, row in spots]
    near_spots = [rows_of(*pair) for pair in (((0, 0), (0, 1)), ((2, 0), (0, 3)), ((1, 1), (2, 1)), ((0, 2), (1, 0)))]
    far_spots = [rows_of(*pair) for pair in (((0, 4), (0, 5)), ((4, 0), (2, 2)), ((3, 1), (4, 1)), ((1, 2), (3, 0)))]

    table = kv_frames.reshape(-1)
    meta = lambda y: jnp.concatenate([jnp.stack([y, my_z]), table])
    parts, near = after((parts, near))
    theirs = attend(meta(1 - my_y), parts, slots, n_y)
    other = shift(theirs, "yh", n_y, 1)
    mine = attend(meta(my_y), parts, slots, n_y)

    def relay(sent):
        if len(sent) == 5:
            stay, to_up, to_down, late_up, late_down = sent
            low, high = up(to_up), down(to_down)
            return stay, low, low, high, high, late_up, late_down
        stay, to_up, next_up, to_down, next_down, late_up, late_down = sent
        return stay, up(to_up), up(next_up), down(to_down), down(next_down), late_up, late_down

    def last(relayed):
        stay, low, low_b, high, high_a, late_up, late_down = relayed
        late_up, late_down = add_relayed(late_up, low, late_down, high)
        return stay, low_b, up(late_up), high_a, down(late_down)

    here = jnp.stack([my_y, my_c])
    mine, far = after((mine, far))
    sent = project(here, mine, other, near, near_spots, part, True)
    far = near[:3] + far + near[3:] + [swap(piece) for piece in far]
    sent = relay(sent)
    sent_far = relay(project(here, mine, other, far, far_spots, part, False))
    out = finish(jnp.stack([my_l, my_x]), gate, last(sent))
    return finish(jnp.stack([1 - my_l, my_x]), gate, last(sent_far), out)


def solution(mesh):
    fine = Mesh(mesh.devices.reshape(2, 4, 4, 2, 2), ("yh", "z", "x", "yl", "c"))
    frame, batch = ("yh", "z"), ("x", "yl", "c")
    act = P(batch, frame, None)
    return jax.shard_map(
        local,
        mesh=fine,
        in_specs=(act, act, act, P(None, batch), P(batch, None), P()),
        out_specs=act,
        check_vma=False,
    )
```

```python
import functools
import math

import jax
import jax.numpy as jnp
from jax import lax
from jax.experimental import pallas as pl
from jax.experimental.pallas import tpu as pltpu
from jax.sharding import Mesh
from jax.sharding import PartitionSpec as P

HEAD_DIM = 128
FRAME = 64
MIB = 1024 * 1024
VMEM = 60 * MIB
NT = (((1,), (1,)), ((), ()))


def params(limit=VMEM):
    return pltpu.CompilerParams(vmem_limit_bytes=limit)


def layout_kernel(q_ref, k_ref, v_ref, o_ref):
    n_y, _, rows, cols = o_ref.shape
    for y in range(n_y):
        for i, ref in enumerate((q_ref, k_ref, v_ref)):
            o_ref[y, i] = ref[:, y * cols : (y + 1) * cols]


def layout(q, k, v, n_y, n_z):
    rows, width = q.shape
    cols = width // (n_y * n_z)
    block = pl.BlockSpec((rows, n_y * cols), lambda i: (0, i))
    return pl.pallas_call(
        layout_kernel,
        grid=(n_z,),
        in_specs=[block] * 3,
        out_specs=pl.BlockSpec((n_y, None, 3, rows, cols), lambda i: (0, i, 0, 0, 0)),
        out_shape=jax.ShapeDtypeStruct((n_y, n_z, 3, rows, cols), q.dtype),
        compiler_params=params(8 * MIB),
        cost_estimate=pl.CostEstimate(flops=0, bytes_accessed=12 * rows * width, transcendentals=0),
    )(q, k, v)


def attend_kernel(meta, q_ref, k_ref, v_ref, o_ref, *, slots):
    blocks, rows, width = q_ref.shape
    per = rows // FRAME
    heads = width // HEAD_DIM
    n_key = slots * FRAME
    scale = 1.0 / math.sqrt(HEAD_DIM)
    lane = lax.broadcasted_iota(jnp.int32, (1, n_key), 1)
    work = []
    for r in range(blocks):
        block = lax.rem(meta[1] + r, blocks)
        for p in range(per):
            base = 2 + ((meta[0] * blocks + block) * per + p) * slots
            bias = jnp.zeros((1, n_key), jnp.float32)
            picks = []
            for s in range(slots):
                g = meta[base + s]
                inside = (lane >= s * FRAME) & (lane < (s + 1) * FRAME)
                bias = jnp.where(inside, jnp.where(g >= 0, 0.0, -1e30), bias)
                g = jnp.maximum(g, 0)
                picks.append((g // per, pl.multiple_of((g % per) * FRAME, FRAME)))
            for h in range(heads):
                work.append((r, p, slice(h * HEAD_DIM, (h + 1) * HEAD_DIM), block, picks, bias))
    scores = []
    for r, p, cols, block, picks, bias in work:
        key = jnp.concatenate([k_ref[b, pl.ds(o, FRAME), cols] for b, o in picks], 0)
        query = q_ref[block, p * FRAME : (p + 1) * FRAME, cols]
        score = lax.dot_general(query, key, NT, preferred_element_type=jnp.float32)
        scores.append(score * scale + bias)
    tops = [jnp.max(s, axis=1, keepdims=True) for s in scores]
    probs = [jnp.exp(s - t) for s, t in zip(scores, tops)]
    denoms = [jnp.sum(p, axis=1, keepdims=True) for p in probs]
    for (r, p, cols, block, picks, bias), prob, denom in zip(work, probs, denoms):
        val = jnp.concatenate([v_ref[b, pl.ds(o, FRAME), cols] for b, o in picks], 0)
        accum = jnp.dot(prob.astype(jnp.bfloat16), val, preferred_element_type=jnp.float32)
        o_ref[r, p * FRAME : (p + 1) * FRAME, cols] = (accum / denom).astype(jnp.bfloat16)


def attend(meta, parts, slots, n_y):
    blocks, _, rows, width = parts.shape
    n_z = blocks // n_y
    whole = lambda which: pl.BlockSpec((blocks, None, rows, width), lambda i, m: (0, which, 0, 0))
    work = n_z * rows * slots * FRAME * width
    return pl.pallas_call(
        functools.partial(attend_kernel, slots=slots),
        grid_spec=pltpu.PrefetchScalarGridSpec(
            num_scalar_prefetch=1,
            grid=(1,),
            in_specs=[
                pl.BlockSpec((n_z, None, rows, width), lambda i, m: (m[0], 0, 0, 0)),
                whole(1),
                whole(2),
            ],
            out_specs=pl.BlockSpec((n_z, rows, width), lambda i, m: (0, 0, 0)),
        ),
        out_shape=jax.ShapeDtypeStruct((n_z, rows, width), jnp.bfloat16),
        compiler_params=params(32 * MIB),
        cost_estimate=pl.CostEstimate(
            flops=work * 4, bytes_accessed=3 * blocks * rows * width * 2, transcendentals=work // HEAD_DIM
        ),
    )(meta, parts, parts, parts)


def project_kernel(meta, mine_ref, other_ref, *refs, spots, n_piece, paired):
    n_x = len(spots)
    pieces, refs = refs[:n_piece], refs[n_piece:]
    outs, (act, w_buf, r_buf, a_sem, w_sem, r_sem) = refs[:-6], refs[-6:]
    if paired:
        stay, up, down, up_late, down_late = outs
        up, up_next, down, down_next = up.at[0], up.at[1], down.at[0], down.at[1]
    else:
        stay, up, up_next, down, down_next, up_late, down_late = outs
    n_z, rows, depth = mine_ref.shape
    tile = w_buf.shape[0] // n_x
    part = tile // 4
    half, core = meta[0], meta[1]
    loads = {}

    def load(x):
        copies = []
        for k in range(4):
            buffer, row = spots[x][k % 2]
            src = pieces[buffer + k // 2 * (n_piece // 2)].at[pl.ds(row, part)]
            row = x * tile + ((core if k < 2 else 1 - core) * 2 + k % 2) * part
            dst = w_buf.at[pl.ds(pl.multiple_of(row, part), part)]
            copies.append(pltpu.make_async_copy(src, dst, w_sem.at[4 * x + k]))
        for copy in copies:
            copy.start()
        loads[x] = copies

    acts = []
    for i, (ref, at) in enumerate(((mine_ref, half), (other_ref, 1 - half))):
        cols = pl.ds(pl.multiple_of(at * depth, 128), depth)
        acts.append(pltpu.make_async_copy(ref, act.at[:, :, cols], a_sem.at[i]))
        acts[-1].start()
    for x in range(n_x):
        load(x)
    for copy in acts:
        copy.wait()

    stores = []
    for late in range(2):
        xs = range(late * n_x // 2, (late + 1) * n_x // 2)
        for x in xs:
            for copy in loads[x]:
                copy.wait()
        left = act[...].reshape(n_z * rows, 2 * depth)
        weight = w_buf[xs[0] * tile : (xs[-1] + 1) * tile]
        total = lax.dot_general(left, weight, NT, preferred_element_type=jnp.float32)
        r_buf[late] = total.astype(r_buf.dtype)
        block = lambda r: r_buf.at[late, pl.ds(r * rows, rows)]
        there = (up_next, down, down_late) if late else (up_late, up, down_next)
        targets = [(block(0), stay.at[:, pl.ds(xs[0] * tile, len(xs) * tile)])]
        targets += [(block(r + 1), ref) for r, ref in enumerate(there)]
        for src, dst in targets:
            copy = pltpu.make_async_copy(src, dst, r_sem.at[len(stores)])
            copy.start()
            stores.append(copy)
    for copy in stores:
        copy.wait()


def project(meta, mine, other, pieces, spots, part, paired):
    n_z, rows, depth = mine.shape
    n_x = len(spots)
    tile = 4 * part
    width = n_x * tile
    shape = lambda *dims: jax.ShapeDtypeStruct(dims, jnp.bfloat16)
    half = shape(rows, width // 2)
    sent = [shape(2, rows, width // 2)] * 2 if paired else [half] * 4
    hbm = pl.BlockSpec(memory_space=pl.ANY)
    return pl.pallas_call(
        functools.partial(project_kernel, spots=spots, n_piece=len(pieces), paired=paired),
        grid_spec=pltpu.PrefetchScalarGridSpec(
            num_scalar_prefetch=1,
            grid=(1,),
            in_specs=[hbm] * (2 + len(pieces)),
            out_specs=[hbm] * (3 + len(sent)),
            scratch_shapes=[
                pltpu.VMEM((n_z, rows, 2 * depth), jnp.bfloat16),
                pltpu.VMEM((width, 2 * depth), jnp.bfloat16),
                pltpu.VMEM((2, n_z * rows, width // 2), jnp.bfloat16),
                pltpu.SemaphoreType.DMA((2,)),
                pltpu.SemaphoreType.DMA((4 * n_x,)),
                pltpu.SemaphoreType.DMA((2 * n_z,)),
            ],
        ),
        out_shape=[shape(rows, width), *sent, half, half],
        compiler_params=params(20 * MIB),
        cost_estimate=pl.CostEstimate(
            flops=4 * n_z * rows * depth * width,
            bytes_accessed=4 * depth * width + 4 * n_z * rows * width,
            transcendentals=0,
        ),
    )(meta, mine, other, *pieces)


def add_kernel(a_ref, x_ref, b_ref, y_ref, oa_ref, ob_ref):
    wide = lambda ref: ref[...].astype(jnp.float32)
    oa_ref[...] = (wide(a_ref) + wide(x_ref)).astype(oa_ref.dtype)
    ob_ref[...] = (wide(b_ref) + wide(y_ref)).astype(ob_ref.dtype)


def add_relayed(a, from_low, b, from_high):
    rows, width = a.shape
    flat = pl.BlockSpec((rows, width), lambda i: (0, 0))
    lead = pl.BlockSpec((None, rows, width), lambda i: (0, 0, 0))
    got = lead if from_low.ndim == 3 else flat
    return pl.pallas_call(
        add_kernel,
        grid=(1,),
        in_specs=[flat, got, flat, got],
        out_specs=[flat, flat],
        out_shape=[jax.ShapeDtypeStruct(a.shape, a.dtype)] * 2,
        compiler_params=params(4 * MIB),
        cost_estimate=pl.CostEstimate(flops=2 * a.size, bytes_accessed=12 * a.size, transcendentals=0),
    )(a, from_low, b, from_high)


def finish_kernel(meta, gate_ref, own, low_b, low_a, high_a, high_b, *refs):
    o_ref, buf, sem = refs[-3:]
    n_x, _, tile = buf.shape
    half = n_x // 2
    wide = lambda value: value.astype(jnp.float32)
    whole = lambda ref: ref[1] if len(ref.shape) == 3 else ref[...]
    low, high = (whole(low_a), whole(low_b)), (whole(high_a), whole(high_b))
    copies = []
    for x in range(n_x):
        late, at = divmod(x, half)
        cols = slice(at * tile, (at + 1) * tile)
        total = wide(own[:, x * tile : (x + 1) * tile]) + wide(low[late][:, cols]) + wide(high[late][:, cols])
        total = total.astype(jnp.bfloat16).astype(jnp.float32)
        place = pl.ds(pl.multiple_of((2 * lax.rem(meta[1] + x, n_x) + meta[0]) * tile, 128), tile)
        buf[x] = (gate_ref[:, place] * total).astype(buf.dtype)
        copies.append(pltpu.make_async_copy(buf.at[x], o_ref.at[0, :, place], sem.at[x]))
        copies[-1].start()
    for copy in copies:
        copy.wait()


def finish(meta, gate, piece, out=None):
    rows, width = piece[0].shape
    n_x = 4
    hbm = pl.BlockSpec(memory_space=pl.ANY)
    whole = lambda array: pl.BlockSpec(array.shape, lambda i, m: (0,) * array.ndim)
    args, specs = [gate, *piece], [whole(array) for array in (gate, *piece)]
    alias = {}
    if out is not None:
        alias = {len(args) + 1: 0}
        args.append(out)
        specs.append(hbm)
    return pl.pallas_call(
        finish_kernel,
        grid_spec=pltpu.PrefetchScalarGridSpec(
            num_scalar_prefetch=1,
            grid=(1,),
            in_specs=specs,
            out_specs=hbm,
            scratch_shapes=[pltpu.VMEM((n_x, rows, width // n_x), jnp.bfloat16), pltpu.SemaphoreType.DMA((n_x,))],
        ),
        out_shape=jax.ShapeDtypeStruct((1, rows, 2 * width), jnp.bfloat16),
        input_output_aliases=alias,
        compiler_params=params(8 * MIB),
        cost_estimate=pl.CostEstimate(flops=4 * rows * width, bytes_accessed=8 * rows * width, transcendentals=0),
    )(meta, *args)


def local(queries, keys, values, out_weight, gate, kv_frames):
    rows, width = queries.shape[1:]
    n_y, n_z, n_l = lax.axis_size("yh"), lax.axis_size("z"), lax.axis_size("yl")
    n = n_y * n_z
    cols = width // n
    slots = kv_frames.shape[1]
    axes = ("yh", "z", "x", "yl", "c")
    my_y, my_z, my_x, my_l, my_c = (lax.axis_index(a).astype(jnp.int32) for a in axes)
    after = lax.optimization_barrier

    def shift(array, axes, size, by):
        return lax.ppermute(array, axes, [(i, (i + by) % size) for i in range(size)])

    up = lambda array: shift(array, "z", n_z, 1)
    down = lambda array: shift(array, "z", n_z, n_z - 1)
    swap = lambda array: shift(array, "c", 2, 1)

    weight = lax.dynamic_slice_in_dim(out_weight, my_z * (n_y * cols), n_y * cols, 0)
    part = weight.shape[1] // 2
    ring, n_x = n_y * n_l, lax.axis_size("x")
    right = lambda *arrays: shift(jnp.concatenate(arrays, 0), "x", n_x, 1)
    left = lambda *arrays: shift(jnp.concatenate(arrays, 0), "x", n_x, n_x - 1)
    lower, upper = weight[:, :part].T, weight[:, part:].T
    lower, upper, queries = after((lower, upper, queries))
    far_l, far_u = shift(lower, ("yh", "yl"), ring, 1), shift(upper, ("yh", "yl"), ring, ring - 1)
    parts = layout(queries[0], keys[0], values[0], n_y, n_z).reshape(n, 3, rows, cols)
    near_l, near_u = right(lower), left(upper)
    parts, far_l, far_u = after((parts, far_l, far_u))
    parts = lax.all_to_all(parts, ("yh", "z"), 0, 0, tiled=True)
    near_l, near_u, lower, upper = after((near_l, near_u, lower, upper))
    held = jnp.concatenate([lower, upper, near_l, near_u, far_l, far_u], 0)
    low, high = right(upper, near_l, far_l), left(lower, near_u, far_u)
    near = [held, low, high]
    near = near + [swap(piece) for piece in near]
    far = [right(far_u, low[2 * part :]), left(far_l, high[2 * part :])]
    rows_of = lambda *spots: [(buffer, row * part) for buffer, row in spots]
    near_spots = [rows_of(*pair) for pair in (((0, 0), (0, 1)), ((2, 0), (0, 3)), ((1, 1), (2, 1)), ((0, 2), (1, 0)))]
    far_spots = [rows_of(*pair) for pair in (((0, 4), (0, 5)), ((4, 0), (2, 2)), ((3, 1), (4, 1)), ((1, 2), (3, 0)))]

    table = kv_frames.reshape(-1)
    meta = lambda y: jnp.concatenate([jnp.stack([y, my_z]), table])
    parts, near = after((parts, near))
    theirs = attend(meta(1 - my_y), parts, slots, n_y)
    other = shift(theirs, "yh", n_y, 1)
    mine = attend(meta(my_y), parts, slots, n_y)

    def relay(sent):
        if len(sent) == 5:
            stay, to_up, to_down, late_up, late_down = sent
            low, high = up(to_up), down(to_down)
            return stay, low, low, high, high, late_up, late_down
        stay, to_up, next_up, to_down, next_down, late_up, late_down = sent
        return stay, up(to_up), up(next_up), down(to_down), down(next_down), late_up, late_down

    def last(relayed):
        stay, low, low_b, high, high_a, late_up, late_down = relayed
        late_up, late_down = add_relayed(late_up, low, late_down, high)
        return stay, low_b, up(late_up), high_a, down(late_down)

    here = jnp.stack([my_y, my_c])
    mine, far = after((mine, far))
    sent = project(here, mine, other, near, near_spots, part, True)
    far = near[:3] + far + near[3:] + [swap(piece) for piece in far]
    sent = relay(sent)
    sent_far = relay(project(here, mine, other, far, far_spots, part, False))
    out = finish(jnp.stack([my_l, my_x]), gate, last(sent))
    return finish(jnp.stack([1 - my_l, my_x]), gate, last(sent_far), out)


def solution(mesh):
    fine = Mesh(mesh.devices.reshape(2, 4, 4, 2, 2), ("yh", "z", "x", "yl", "c"))
    frame, batch = ("yh", "z"), ("x", "yl", "c")
    act = P(batch, frame, None)
    return jax.shard_map(
        local,
        mesh=fine,
        in_specs=(act, act, act, P(None, batch), P(batch, None), P()),
        out_specs=act,
        check_vma=False,
    )
```

```python
import functools
import math

import jax
import jax.numpy as jnp
from jax import lax
from jax.experimental import pallas as pl
from jax.experimental.pallas import tpu as pltpu
from jax.sharding import Mesh
from jax.sharding import PartitionSpec as P

HEAD_DIM = 128
FRAME = 64
MIB = 1024 * 1024
VMEM = 60 * MIB
NT = (((1,), (1,)), ((), ()))


def params(limit=VMEM):
    return pltpu.CompilerParams(vmem_limit_bytes=limit)


def layout_kernel(q_ref, k_ref, v_ref, o_ref):
    n_y, _, rows, cols = o_ref.shape
    for y in range(n_y):
        for i, ref in enumerate((q_ref, k_ref, v_ref)):
            o_ref[y, i] = ref[:, y * cols : (y + 1) * cols]


def layout(q, k, v, n_y, n_z):
    rows, width = q.shape
    cols = width // (n_y * n_z)
    block = pl.BlockSpec((rows, n_y * cols), lambda i: (0, i))
    return pl.pallas_call(
        layout_kernel,
        grid=(n_z,),
        in_specs=[block] * 3,
        out_specs=pl.BlockSpec((n_y, None, 3, rows, cols), lambda i: (0, i, 0, 0, 0)),
        out_shape=jax.ShapeDtypeStruct((n_y, n_z, 3, rows, cols), q.dtype),
        compiler_params=params(8 * MIB),
        cost_estimate=pl.CostEstimate(flops=0, bytes_accessed=12 * rows * width, transcendentals=0),
    )(q, k, v)


def attend_kernel(meta, parts_ref, o_ref, q_ref, k_ref, v_ref, sem, *, slots, groups):
    blocks, rows, width = q_ref.shape
    per = rows // FRAME
    n_key = slots * FRAME
    scale = 1.0 / math.sqrt(HEAD_DIM)
    loads, at = [], 0
    for n, group in enumerate(groups):
        cols = pl.ds(at * HEAD_DIM, group * HEAD_DIM)
        mine = parts_ref.at[pl.ds(meta[0] * blocks, blocks), 0, :, cols]
        copies = [pltpu.make_async_copy(mine, q_ref.at[:, :, cols], sem.at[3 * n])]
        for which, ref in ((1, k_ref), (2, v_ref)):
            source = parts_ref.at[:, which, :, cols]
            copies.append(pltpu.make_async_copy(source, ref.at[:, :, cols], sem.at[3 * n + which]))
        for copy in copies:
            copy.start()
        loads.append((copies, range(at, at + group)))
        at += group

    lane = lax.broadcasted_iota(jnp.int32, (1, n_key), 1)
    frames = []
    for r in range(blocks):
        block = lax.rem(meta[1] + r, blocks)
        for p in range(per):
            base = 2 + ((meta[0] * blocks + block) * per + p) * slots
            bias = jnp.zeros((1, n_key), jnp.float32)
            picks = []
            for s in range(slots):
                g = meta[base + s]
                inside = (lane >= s * FRAME) & (lane < (s + 1) * FRAME)
                bias = jnp.where(inside, jnp.where(g >= 0, 0.0, -1e30), bias)
                g = jnp.maximum(g, 0)
                picks.append((g // per, pl.multiple_of((g % per) * FRAME, FRAME)))
            frames.append((r, p, block, picks, bias))
    for copies, heads in loads:
        for copy in copies:
            copy.wait()
        work = [(*frame, slice(h * HEAD_DIM, (h + 1) * HEAD_DIM)) for frame in frames for h in heads]
        scores = []
        for r, p, block, picks, bias, cols in work:
            key = jnp.concatenate([k_ref[b, pl.ds(o, FRAME), cols] for b, o in picks], 0)
            query = q_ref[block, p * FRAME : (p + 1) * FRAME, cols]
            score = lax.dot_general(query, key, NT, preferred_element_type=jnp.float32)
            scores.append(score * scale + bias)
        tops = [jnp.max(s, axis=1, keepdims=True) for s in scores]
        probs = [jnp.exp(s - t) for s, t in zip(scores, tops)]
        denoms = [jnp.sum(p, axis=1, keepdims=True) for p in probs]
        for (r, p, block, picks, bias, cols), prob, denom in zip(work, probs, denoms):
            val = jnp.concatenate([v_ref[b, pl.ds(o, FRAME), cols] for b, o in picks], 0)
            accum = jnp.dot(prob.astype(jnp.bfloat16), val, preferred_element_type=jnp.float32)
            o_ref[r, p * FRAME : (p + 1) * FRAME, cols] = (accum / denom).astype(jnp.bfloat16)


def attend(meta, parts, slots, n_y):
    blocks, _, rows, width = parts.shape
    n_z = blocks // n_y
    work = n_z * rows * slots * FRAME * width
    groups = (2, 3)
    return pl.pallas_call(
        functools.partial(attend_kernel, slots=slots, groups=groups),
        grid_spec=pltpu.PrefetchScalarGridSpec(
            num_scalar_prefetch=1,
            grid=(1,),
            in_specs=[pl.BlockSpec(memory_space=pl.ANY)],
            out_specs=pl.BlockSpec((n_z, rows, width), lambda i, m: (0, 0, 0)),
            scratch_shapes=[
                pltpu.VMEM((n_z, rows, width), jnp.bfloat16),
                pltpu.VMEM((blocks, rows, width), jnp.bfloat16),
                pltpu.VMEM((blocks, rows, width), jnp.bfloat16),
                pltpu.SemaphoreType.DMA((3 * len(groups),)),
            ],
        ),
        out_shape=jax.ShapeDtypeStruct((n_z, rows, width), jnp.bfloat16),
        compiler_params=params(32 * MIB),
        cost_estimate=pl.CostEstimate(
            flops=work * 4, bytes_accessed=3 * blocks * rows * width * 2, transcendentals=work // HEAD_DIM
        ),
    )(meta, parts)


def project_kernel(meta, mine_ref, other_ref, *refs, spots, n_piece, paired):
    n_x = len(spots)
    pieces, refs = refs[:n_piece], refs[n_piece:]
    outs, (act, w_buf, r_buf, a_sem, w_sem, r_sem) = refs[:-6], refs[-6:]
    if paired:
        stay, up, down, up_late, down_late = outs
        up, up_next, down, down_next = up.at[0], up.at[1], down.at[0], down.at[1]
    else:
        stay, up, up_next, down, down_next, up_late, down_late = outs
    n_z, rows, depth = mine_ref.shape
    tile = w_buf.shape[0] // n_x
    part = tile // 4
    half, core = meta[0], meta[1]
    loads = {}

    def load(x):
        copies = []
        for k in range(4):
            buffer, row = spots[x][k % 2]
            src = pieces[buffer + k // 2 * (n_piece // 2)].at[pl.ds(row, part)]
            row = x * tile + ((core if k < 2 else 1 - core) * 2 + k % 2) * part
            dst = w_buf.at[pl.ds(pl.multiple_of(row, part), part)]
            copies.append(pltpu.make_async_copy(src, dst, w_sem.at[4 * x + k]))
        for copy in copies:
            copy.start()
        loads[x] = copies

    acts = []
    for i, (ref, at) in enumerate(((mine_ref, half), (other_ref, 1 - half))):
        cols = pl.ds(pl.multiple_of(at * depth, 128), depth)
        acts.append(pltpu.make_async_copy(ref, act.at[:, :, cols], a_sem.at[i]))
        acts[-1].start()
    for x in range(n_x):
        load(x)
    for copy in acts:
        copy.wait()

    stores = []
    for late in range(2):
        xs = range(late * n_x // 2, (late + 1) * n_x // 2)
        for x in xs:
            for copy in loads[x]:
                copy.wait()
        left = act[...].reshape(n_z * rows, 2 * depth)
        weight = w_buf[xs[0] * tile : (xs[-1] + 1) * tile]
        total = lax.dot_general(left, weight, NT, preferred_element_type=jnp.float32)
        r_buf[late] = total.astype(r_buf.dtype)
        block = lambda r: r_buf.at[late, pl.ds(r * rows, rows)]
        there = (up_next, down, down_late) if late else (up_late, up, down_next)
        targets = [(block(0), stay.at[:, pl.ds(xs[0] * tile, len(xs) * tile)])]
        targets += [(block(r + 1), ref) for r, ref in enumerate(there)]
        for src, dst in targets:
            copy = pltpu.make_async_copy(src, dst, r_sem.at[len(stores)])
            copy.start()
            stores.append(copy)
    for copy in stores:
        copy.wait()


def project(meta, mine, other, pieces, spots, part, paired):
    n_z, rows, depth = mine.shape
    n_x = len(spots)
    tile = 4 * part
    width = n_x * tile
    shape = lambda *dims: jax.ShapeDtypeStruct(dims, jnp.bfloat16)
    half = shape(rows, width // 2)
    sent = [shape(2, rows, width // 2)] * 2 if paired else [half] * 4
    hbm = pl.BlockSpec(memory_space=pl.ANY)
    return pl.pallas_call(
        functools.partial(project_kernel, spots=spots, n_piece=len(pieces), paired=paired),
        grid_spec=pltpu.PrefetchScalarGridSpec(
            num_scalar_prefetch=1,
            grid=(1,),
            in_specs=[hbm] * (2 + len(pieces)),
            out_specs=[hbm] * (3 + len(sent)),
            scratch_shapes=[
                pltpu.VMEM((n_z, rows, 2 * depth), jnp.bfloat16),
                pltpu.VMEM((width, 2 * depth), jnp.bfloat16),
                pltpu.VMEM((2, n_z * rows, width // 2), jnp.bfloat16),
                pltpu.SemaphoreType.DMA((2,)),
                pltpu.SemaphoreType.DMA((4 * n_x,)),
                pltpu.SemaphoreType.DMA((2 * n_z,)),
            ],
        ),
        out_shape=[shape(rows, width), *sent, half, half],
        compiler_params=params(20 * MIB),
        cost_estimate=pl.CostEstimate(
            flops=4 * n_z * rows * depth * width,
            bytes_accessed=4 * depth * width + 4 * n_z * rows * width,
            transcendentals=0,
        ),
    )(meta, mine, other, *pieces)


def add_kernel(a_ref, x_ref, b_ref, y_ref, oa_ref, ob_ref):
    wide = lambda ref: ref[...].astype(jnp.float32)
    oa_ref[...] = (wide(a_ref) + wide(x_ref)).astype(oa_ref.dtype)
    ob_ref[...] = (wide(b_ref) + wide(y_ref)).astype(ob_ref.dtype)


def add_relayed(a, from_low, b, from_high):
    rows, width = a.shape
    flat = pl.BlockSpec((rows, width), lambda i: (0, 0))
    lead = pl.BlockSpec((None, rows, width), lambda i: (0, 0, 0))
    got = lead if from_low.ndim == 3 else flat
    return pl.pallas_call(
        add_kernel,
        grid=(1,),
        in_specs=[flat, got, flat, got],
        out_specs=[flat, flat],
        out_shape=[jax.ShapeDtypeStruct(a.shape, a.dtype)] * 2,
        compiler_params=params(4 * MIB),
        cost_estimate=pl.CostEstimate(flops=2 * a.size, bytes_accessed=12 * a.size, transcendentals=0),
    )(a, from_low, b, from_high)


def finish_kernel(meta, gate_ref, own, low_b, low_a, high_a, high_b, *refs):
    o_ref, buf, sem = refs[-3:]
    n_x, _, tile = buf.shape
    half = n_x // 2
    wide = lambda value: value.astype(jnp.float32)
    whole = lambda ref: ref[1] if len(ref.shape) == 3 else ref[...]
    low, high = (whole(low_a), whole(low_b)), (whole(high_a), whole(high_b))
    copies = []
    for x in range(n_x):
        late, at = divmod(x, half)
        cols = slice(at * tile, (at + 1) * tile)
        total = wide(own[:, x * tile : (x + 1) * tile]) + wide(low[late][:, cols]) + wide(high[late][:, cols])
        total = total.astype(jnp.bfloat16).astype(jnp.float32)
        place = pl.ds(pl.multiple_of((2 * lax.rem(meta[1] + x, n_x) + meta[0]) * tile, 128), tile)
        buf[x] = (gate_ref[:, place] * total).astype(buf.dtype)
        copies.append(pltpu.make_async_copy(buf.at[x], o_ref.at[0, :, place], sem.at[x]))
        copies[-1].start()
    for copy in copies:
        copy.wait()


def finish(meta, gate, piece, out=None):
    rows, width = piece[0].shape
    n_x = 4
    hbm = pl.BlockSpec(memory_space=pl.ANY)
    whole = lambda array: pl.BlockSpec(array.shape, lambda i, m: (0,) * array.ndim)
    args, specs = [gate, *piece], [whole(array) for array in (gate, *piece)]
    alias = {}
    if out is not None:
        alias = {len(args) + 1: 0}
        args.append(out)
        specs.append(hbm)
    return pl.pallas_call(
        finish_kernel,
        grid_spec=pltpu.PrefetchScalarGridSpec(
            num_scalar_prefetch=1,
            grid=(1,),
            in_specs=specs,
            out_specs=hbm,
            scratch_shapes=[pltpu.VMEM((n_x, rows, width // n_x), jnp.bfloat16), pltpu.SemaphoreType.DMA((n_x,))],
        ),
        out_shape=jax.ShapeDtypeStruct((1, rows, 2 * width), jnp.bfloat16),
        input_output_aliases=alias,
        compiler_params=params(8 * MIB),
        cost_estimate=pl.CostEstimate(flops=4 * rows * width, bytes_accessed=8 * rows * width, transcendentals=0),
    )(meta, *args)


def local(queries, keys, values, out_weight, gate, kv_frames):
    rows, width = queries.shape[1:]
    n_y, n_z, n_l = lax.axis_size("yh"), lax.axis_size("z"), lax.axis_size("yl")
    n = n_y * n_z
    cols = width // n
    slots = kv_frames.shape[1]
    axes = ("yh", "z", "x", "yl", "c")
    my_y, my_z, my_x, my_l, my_c = (lax.axis_index(a).astype(jnp.int32) for a in axes)
    after = lax.optimization_barrier

    def shift(array, axes, size, by):
        return lax.ppermute(array, axes, [(i, (i + by) % size) for i in range(size)])

    up = lambda array: shift(array, "z", n_z, 1)
    down = lambda array: shift(array, "z", n_z, n_z - 1)
    swap = lambda array: shift(array, "c", 2, 1)

    weight = lax.dynamic_slice_in_dim(out_weight, my_z * (n_y * cols), n_y * cols, 0)
    part = weight.shape[1] // 2
    ring, n_x = n_y * n_l, lax.axis_size("x")
    right = lambda *arrays: shift(jnp.concatenate(arrays, 0), "x", n_x, 1)
    left = lambda *arrays: shift(jnp.concatenate(arrays, 0), "x", n_x, n_x - 1)
    lower, upper = weight[:, :part].T, weight[:, part:].T
    lower, upper, queries = after((lower, upper, queries))
    far_l, far_u = shift(lower, ("yh", "yl"), ring, 1), shift(upper, ("yh", "yl"), ring, ring - 1)
    parts = layout(queries[0], keys[0], values[0], n_y, n_z).reshape(n, 3, rows, cols)
    near_l, near_u = right(lower), left(upper)
    parts, far_l, far_u = after((parts, far_l, far_u))
    parts = lax.all_to_all(parts, ("yh", "z"), 0, 0, tiled=True)
    near_l, near_u, lower, upper = after((near_l, near_u, lower, upper))
    held = jnp.concatenate([lower, upper, near_l, near_u, far_l, far_u], 0)
    low, high = right(upper, near_l, far_l), left(lower, near_u, far_u)
    near = [held, low, high]
    near = near + [swap(piece) for piece in near]
    far = [right(far_u, low[2 * part :]), left(far_l, high[2 * part :])]
    rows_of = lambda *spots: [(buffer, row * part) for buffer, row in spots]
    near_spots = [rows_of(*pair) for pair in (((0, 0), (0, 1)), ((2, 0), (0, 3)), ((1, 1), (2, 1)), ((0, 2), (1, 0)))]
    far_spots = [rows_of(*pair) for pair in (((0, 4), (0, 5)), ((4, 0), (2, 2)), ((3, 1), (4, 1)), ((1, 2), (3, 0)))]

    table = kv_frames.reshape(-1)
    meta = lambda y: jnp.concatenate([jnp.stack([y, my_z]), table])
    parts, near = after((parts, near))
    theirs = attend(meta(1 - my_y), parts, slots, n_y)
    other = shift(theirs, "yh", n_y, 1)
    mine = attend(meta(my_y), parts, slots, n_y)

    def relay(sent):
        if len(sent) == 5:
            stay, to_up, to_down, late_up, late_down = sent
            low, high = up(to_up), down(to_down)
            return stay, low, low, high, high, late_up, late_down
        stay, to_up, next_up, to_down, next_down, late_up, late_down = sent
        return stay, up(to_up), up(next_up), down(to_down), down(next_down), late_up, late_down

    def last(relayed):
        stay, low, low_b, high, high_a, late_up, late_down = relayed
        late_up, late_down = add_relayed(late_up, low, late_down, high)
        return stay, low_b, up(late_up), high_a, down(late_down)

    here = jnp.stack([my_y, my_c])
    mine, far = after((mine, far))
    sent = project(here, mine, other, near, near_spots, part, True)
    far = near[:3] + far + near[3:] + [swap(piece) for piece in far]
    sent = relay(sent)
    sent_far = relay(project(here, mine, other, far, far_spots, part, False))
    out = finish(jnp.stack([my_l, my_x]), gate, last(sent))
    return finish(jnp.stack([1 - my_l, my_x]), gate, last(sent_far), out)


def solution(mesh):
    fine = Mesh(mesh.devices.reshape(2, 4, 4, 2, 2), ("yh", "z", "x", "yl", "c"))
    frame, batch = ("yh", "z"), ("x", "yl", "c")
    act = P(batch, frame, None)
    return jax.shard_map(
        local,
        mesh=fine,
        in_specs=(act, act, act, P(None, batch), P(batch, None), P()),
        out_specs=act,
        check_vma=False,
    )
```
